32 devices in a mesh: dp: 4 (over z), seq: 4 (over x, core), index: 2 (over y).
Axes of the slice: x: 2, y: 2, z: 4, core: 2. Of those that a mesh axis runs over, the one named last changes fastest.
Arguments:
- hidden: bfloat16 [4, 1024, 2048], P('dp', 'seq'), may hold values from -32 to 32
- proj_weight: bfloat16 [4, 2048, 1536], P(None, 'dp', 'index')
- stretch_lengths: int32 [4, 32], P('dp'), may hold values from 1 to 512, 1024 in all within a row
- shard_of: int32 [4, 32, 1], P('dp', 'seq'), may hold values from 0 to 1; in each aligned block of 8 rows (0 to 7, 8 to 15, ..., all dimensions but the last counted through in order) at most 4 rows name the same one
Outputs:
- layer_out: bfloat16 [4, 1024, 2048], P('dp', 'seq', 'index')
- shelf: float32 [4, 4, 2, 4, 2048], P('dp', 'seq', 'index')
The draws below stay inside these ranges and needn't reach their ends.
Inputs may be any that keep to these rules, and one draw needn't show every extreme that they name: `stretch_lengths`: the 32 lengths of a manual sum to 1024; the largest is 512. `shard_of`: in each aligned block of 8 rows of a manual no shard is named more than 4 times, a bound that some block reaches.
All inputs are finite; a program needn't handle non-finite values.
Results may differ from the reference program's by a relative error of at most 0.01.
Values may be sent and summed in bfloat16 or wider, within the bound.
No kernel may reach another device: no remote copies, remote signals or barrier semaphores. Data moves between devices by JAX's collectives and lax.ppermute only.
A program may use at most 64 MiB of HBM per device.

```python
import math
import jax
import jax.numpy as jnp
import numpy as np
from jax import lax

D = 2048
HEADS = 24
HD = 64
HALF_WIN = 256
CH_MOST = 512
STRETCHES = 32
MANUALS = 4
LENGTH = 1024
BLOCKS = 4
HEAD_GROUPS = 2
CH_DEV = 8
CAP = 4


def draw_hidden(key, part):
    shape = (MANUALS, LENGTH, D)
    first = jax.random.fold_in(key, 0)
    values = jnp.clip(jax.random.normal(first, shape, jnp.float32), -6.0, 6.0)
    return jnp.clip(values, -32.0, 32.0).astype(jnp.bfloat16)


def draw_proj_weight(key, part):
    shape = (4, D, HEADS * HD)
    first = jax.random.fold_in(key, 0)
    values = jnp.clip(jax.random.normal(first, shape, jnp.float32), -4.0, 4.0)
    return (values * D ** (-0.5)).astype(jnp.bfloat16)


def profile(count, total, bound, lean):
    portions = [(1 << 20) // math.isqrt(rank ** lean) + 1 for rank in range(2, count + 1)]
    surplus, holding = total - bound - (count - 1), [1] * (count - 1)
    while surplus > 0:
        movable = [i for i in range(count - 1) if holding[i] < bound]
        mass, left = sum([portions[i] for i in movable]), surplus
        for i in movable:
            addition = min(bound - holding[i], max(1, left * portions[i] // mass), surplus)
            holding[i] = holding[i] + addition
            surplus = surplus - addition
    return np.array([bound] + holding)


def ragged(stream_key, amount, total, limit, lean):
    if amount == 2:
        one = jax.random.randint(stream_key, (), max(1, total - limit), min(limit, total - 1) + 1)
        return jnp.stack([one, total - one])
    sizes = jnp.asarray(profile(amount, total, limit, lean), jnp.int32)
    twos = (amount - 1) // 2
    giver, taker = sizes[1:1 + 2 * twos:2], sizes[2:2 + 2 * twos:2]
    margin = jnp.minimum(giver - 1, limit - taker)
    moved = jax.random.randint(jax.random.fold_in(stream_key, 1), (twos,), 0, 1 << 20) % (margin + 1)
    sizes = sizes.at[1:1 + 2 * twos:2].set(giver - moved).at[2:2 + 2 * twos:2].set(taker + moved)
    return sizes[jax.random.permutation(jax.random.fold_in(stream_key, 2), amount)]


def shared_out(stream_key, own, number, rows, amount, top, reach, lean):
    order = jax.random.permutation(stream_key, amount)
    packed, usual = portions_of(amount, rows * top, reach, lean, True), portions_of(amount, rows * top, reach, lean, False)
    places = jnp.arange(amount)

    def named(sizes, offset_by):
        used = int((sizes > 0).sum())
        fixed = max(1, used // 4)
        moved = fixed + (places - fixed + offset_by * (used - fixed)) % max(1, amount - fixed)
        return jnp.zeros((amount,), jnp.int32).at[order[jnp.where(places < fixed, places, moved)]].set(jnp.asarray(sizes, jnp.int32))

    sizes = jnp.where(number % 4 == 0, named(packed, number // 4), named(usual, number - number // 4 - 1))
    mixed = jax.random.permutation(jax.random.fold_in(own, 3), amount)
    donor, taker = mixed[0:amount // 2 * 2:2], mixed[1:amount // 2 * 2:2]
    room = jnp.minimum(sizes[donor] - 1, reach - sizes[taker]) // 2
    room = jnp.where((donor == order[0]) | (taker == order[0]) | (sizes[taker] == 0), 0, jnp.maximum(room, 0))
    moved = jax.random.randint(jax.random.fold_in(own, 4), (amount // 2,), 0, 1 << 20) % (room + 1)
    sizes = sizes.at[donor].add(-moved).at[taker].add(moved)
    items = jnp.searchsorted(jnp.cumsum(sizes), jnp.arange(rows * top), side="right").astype(jnp.int32)
    table = items.reshape(top, rows).T
    table = table[jax.random.permutation(jax.random.fold_in(own, 1), rows)]
    offset_by = jax.random.randint(jax.random.fold_in(own, 2), (rows, 1), 0, top)
    return jnp.take_along_axis(table, (jnp.arange(top)[None, :] + offset_by) % top, axis=1)


def portions_of(number_of, total, reach, skew, full):
    weights = [(1 << 20) // math.isqrt(rank ** skew) + 1 for rank in range(1, number_of + 1)]
    largest = reach if full else min(reach, max(-(-total // number_of), total * weights[0] // sum(weights)))
    least = 1 if total - largest >= number_of - 1 else 0
    counts, surplus = [largest] + [least] * (number_of - 1), total - largest - least * (number_of - 1)
    while surplus > 0:
        movable = [i for i in range(1, number_of) if counts[i] < largest] or [i for i in range(1, number_of) if counts[i] < reach]
        mass, left = sum([weights[i] for i in movable]), surplus
        for i in movable:
            more = min(reach - counts[i], max(1, left * weights[i] // mass), surplus)
            counts[i] = counts[i] + more
            surplus = surplus - more
    return np.array(counts)


def setup_inputs(seed: int = 0) -> dict:
    keys = jax.random.split(jax.random.key(seed), 5)
    hidden = draw_hidden(jax.random.fold_in(keys[4], 71), 0)
    proj_weight = draw_proj_weight(jax.random.fold_in(keys[4], 71), 0)
    stretch_lengths = jax.vmap(lambda own: ragged(own, STRETCHES, LENGTH, CH_MOST, 2))(jax.random.split(keys[2], MANUALS)).reshape((MANUALS, STRETCHES)).astype(jnp.int32)
    shard_of_keys = jax.random.split(jax.random.fold_in(keys[3], 1), MANUALS * STRETCHES // CH_DEV)
    shard_of_turns = jax.random.permutation(jax.random.fold_in(keys[3], 3), MANUALS * STRETCHES // CH_DEV)
    shard_of = jax.vmap(lambda own, number: shared_out(jax.random.fold_in(keys[3], 2), own, number, CH_DEV, HEAD_GROUPS, 1, CAP, 2))(shard_of_keys, shard_of_turns).reshape((MANUALS, STRETCHES, 1))
    return dict(hidden=hidden, proj_weight=proj_weight, stretch_lengths=stretch_lengths, shard_of=shard_of)


def rotate(values_in, positions):
    half_dim = HD // 2
    freqs = 10000.0 ** (-2.0 * jnp.arange(half_dim, dtype=jnp.float32) / HD)
    angles = positions.astype(jnp.float32)[:, None] * freqs[None, :]
    cosine = jnp.cos(angles)[:, None, :]
    sine = jnp.sin(angles)[:, None, :]
    first = values_in[..., :half_dim]
    second = values_in[..., half_dim:]
    return jnp.concatenate([first * cosine - second * sine, second * cosine + first * sine], -1)

def window_heads(queries, key_rows, value_rows, visible):
    scale = HD ** (-0.5)

    def one_head(items):
        query_head, key_head, value_head = items
        scores = jnp.dot(query_head, key_head.T, preferred_element_type=jnp.float32) * scale
        scores = jnp.where(visible, scores, -1e+30)
        maxima = lax.optimization_barrier(jnp.max(scores, -1, keepdims=True))
        expo = jnp.exp(scores - maxima)
        weights = (expo / lax.optimization_barrier(jnp.sum(expo, -1, keepdims=True))).astype(jnp.bfloat16)
        return jnp.dot(weights, value_head, preferred_element_type=jnp.float32).astype(jnp.bfloat16)
    context = lax.map(one_head, (jnp.moveaxis(queries, 1, 0), jnp.moveaxis(key_rows, 1, 0), jnp.moveaxis(value_rows, 1, 0)))
    return jnp.moveaxis(context, 0, 1)

def attend_manual(queries, key_rows, value_rows):
    block = min(512, LENGTH)
    count = LENGTH // block
    padding = ((HALF_WIN, HALF_WIN), (0, 0), (0, 0))
    key_pad = jnp.pad(key_rows, padding)
    value_pad = jnp.pad(value_rows, padding)
    span = block + 2 * HALF_WIN

    def one_block(index_block):
        offset = index_block * block
        query_part = lax.dynamic_slice_in_dim(queries, offset, block, 0)
        key_part = lax.dynamic_slice_in_dim(key_pad, offset, span, 0)
        value_part = lax.dynamic_slice_in_dim(value_pad, offset, span, 0)
        query_pos = offset + jnp.arange(block, dtype=jnp.int32)
        key_pos = offset - HALF_WIN + jnp.arange(span, dtype=jnp.int32)
        visible = (jnp.abs(key_pos[None, :] - query_pos[:, None]) <= HALF_WIN) & (key_pos[None, :] >= 0) & (key_pos[None, :] < LENGTH)
        return window_heads(query_part, key_part, value_part, visible)
    blocks_out = lax.map(one_block, jnp.arange(count, dtype=jnp.int32))
    return blocks_out.reshape(LENGTH, HEADS, HD)

def reference(hidden, proj_weight, stretch_lengths, shard_of):
    width = HEADS // HEAD_GROUPS * HD

    def one_manual(items):
        states, lengths, shards = items
        positions = jnp.arange(LENGTH, dtype=jnp.int32)
        projected = [jnp.dot(states, proj_weight[j], preferred_element_type=jnp.float32) for j in range(3)]
        queries = rotate(projected[0].reshape(LENGTH, HEADS, HD), positions).astype(jnp.bfloat16)
        key_rows = rotate(projected[1].reshape(LENGTH, HEADS, HD), positions).astype(jnp.bfloat16)
        value_rows = projected[2].reshape(LENGTH, HEADS, HD).astype(jnp.bfloat16)
        context = attend_manual(queries, key_rows, value_rows).reshape(LENGTH, HEADS * HD)
        running = states.astype(jnp.float32)
        for group_index in range(HEAD_GROUPS):
            cols = slice(group_index * width, (group_index + 1) * width)
            partial_value = jnp.dot(context[:, cols], proj_weight[3][:, cols].T, preferred_element_type=jnp.float32).astype(jnp.bfloat16)
            running = running + partial_value.astype(jnp.float32)
        layer = running.astype(jnp.bfloat16)
        ends = jnp.cumsum(lengths, dtype=jnp.int32)
        starts = ends - lengths
        row_ids = jnp.arange(STRETCHES, dtype=jnp.int32)
        order = (row_ids % CH_DEV * BLOCKS + row_ids // CH_DEV).astype(jnp.int32)
        row_starts = starts[order]
        row_ends = ends[order]
        member = ((positions[None, :] >= row_starts[:, None]) & (positions[None, :] < row_ends[:, None])).astype(jnp.bfloat16)
        pooled = jnp.dot(member, layer, preferred_element_type=jnp.float32)
        embedded = pooled * lax.rsqrt(lax.optimization_barrier(jnp.mean(pooled * pooled, -1, keepdims=True)) + 1e-06)
        shard_ids = shards[:, 0].astype(jnp.int32)
        block_ids = row_ids // CH_DEV
        earlier = (shard_ids[:, None] == shard_ids[None, :]) & (block_ids[:, None] == block_ids[None, :]) & (row_ids[None, :] < row_ids[:, None])
        slot_rank = lax.optimization_barrier(jnp.sum(earlier.astype(jnp.int32), 1)).astype(jnp.int32)
        place = (block_ids * HEAD_GROUPS + shard_ids) * CAP + slot_rank
        targets = jnp.arange(BLOCKS * HEAD_GROUPS * CAP, dtype=jnp.int32)
        onehot = (place[None, :] == targets[:, None]).astype(jnp.float32)
        shelf_rows = jnp.dot(onehot, embedded, precision=lax.Precision.HIGHEST)
        return (layer, shelf_rows.reshape(BLOCKS, HEAD_GROUPS, CAP, D))
    layer_out, shelf = lax.map(one_manual, (hidden, stretch_lengths, shard_of))
    return (layer_out, shelf)
```

```python
import functools

import jax
import jax.numpy as jnp
from jax import lax
from jax.experimental import pallas as pl
from jax.experimental.pallas import tpu as pltpu
from jax.sharding import PartitionSpec as P

D = 2048
HD = 64
HALF_WIN = 256


def with_halo(cells, sides, width):
    for axis, dim in sides:
        count = lax.axis_size(axis)
        ends = count - 1
        head = lax.slice_in_dim(cells, 0, width, axis=dim)
        tail = lax.slice_in_dim(cells, cells.shape[dim] - width, cells.shape[dim], axis=dim)
        cells = jnp.concatenate(
            [
                lax.ppermute(tail, axis, [(i, (i + 1) % count) for i in range(ends)]),
                cells,
                lax.ppermute(head, axis, [((i + 1) % count, i) for i in range(ends)]),
            ],
            axis=dim,
        )
    return cells


def rotate(values_in, positions):
    half_dim = HD // 2
    freqs = 10000.0 ** (-2.0 * jnp.arange(half_dim, dtype=jnp.float32) / HD)
    angles = positions.astype(jnp.float32)[:, None] * freqs[None, :]
    cosine = jnp.cos(angles)[:, None, :]
    sine = jnp.sin(angles)[:, None, :]
    first = values_in[..., :half_dim]
    second = values_in[..., half_dim:]
    return jnp.concatenate([first * cosine - second * sine, second * cosine + first * sine], -1)


def window_heads(queries, key_rows, value_rows, visible):
    scale = HD ** (-0.5)

    def one_head(items):
        query_head, key_head, value_head = items
        scores = jnp.dot(query_head, key_head.T, preferred_element_type=jnp.float32) * scale
        scores = jnp.where(visible, scores, -1e30)
        maxima = jnp.max(scores, -1, keepdims=True)
        expo = jnp.exp(scores - maxima)
        weights = (expo / jnp.sum(expo, -1, keepdims=True)).astype(jnp.bfloat16)
        return jnp.dot(weights, value_head, preferred_element_type=jnp.float32).astype(jnp.bfloat16)

    context = lax.map(
        one_head,
        (jnp.moveaxis(queries, 1, 0), jnp.moveaxis(key_rows, 1, 0), jnp.moveaxis(value_rows, 1, 0)),
    )
    return jnp.moveaxis(context, 0, 1)


def body(hidden, proj_weight, stretch_lengths, shard_of):
    states = hidden[0]
    tokens_here = states.shape[0]
    width = proj_weight.shape[2]
    heads_here = width // HD
    seq_index = lax.axis_index("seq")
    group_index = lax.axis_index("index")
    seq_count = lax.axis_size("seq")
    index_count = lax.axis_size("index")
    total_length = tokens_here * seq_count
    positions = seq_index * tokens_here + jnp.arange(tokens_here, dtype=jnp.int32)
    projected = jnp.einsum(
        "td,jdc->jtc",
        states,
        lax.all_gather(proj_weight[:3], "dp", axis=1, tiled=True),
        preferred_element_type=jnp.float32,
    )
    queries = rotate(projected[0].reshape(tokens_here, heads_here, HD), positions).astype(
        jnp.bfloat16
    )
    key_rows = rotate(projected[1].reshape(tokens_here, heads_here, HD), positions).astype(
        jnp.bfloat16
    )
    value_rows = projected[2].astype(jnp.bfloat16)
    stacked = jnp.stack([key_rows.reshape(tokens_here, width), value_rows])
    padded = with_halo(stacked, (("seq", 1),), HALF_WIN)
    span = tokens_here + 2 * HALF_WIN
    key_part = padded[0, 0:span].reshape(span, heads_here, HD)
    value_part = padded[1, 0:span].reshape(span, heads_here, HD)
    key_pos = seq_index * tokens_here + 0 - HALF_WIN + jnp.arange(span, dtype=jnp.int32)
    visible = (
        (jnp.abs(key_pos[None, :] - positions[:, None]) <= HALF_WIN)
        & (key_pos[None, :] >= 0)
        & (key_pos[None, :] < total_length)
    )
    context_parts = window_heads(queries, key_part, value_part, visible).reshape(tokens_here, width)
    partial_value = lax.dot_general(
        context_parts,
        lax.all_gather(proj_weight[3], "dp", axis=0, tiled=True),
        (((1,), (1,)), ((), ())),
        preferred_element_type=jnp.float32,
    )
    lengths = stretch_lengths[0]
    stretch_count = lengths.shape[0]
    per_block = stretch_count // seq_count
    ends = jnp.cumsum(lengths, dtype=jnp.int32)
    starts = ends - lengths
    row_ids = jnp.arange(stretch_count, dtype=jnp.int32)
    order = row_ids % per_block * seq_count + row_ids // per_block
    row_starts = starts[order]
    row_ends = ends[order]
    member = (
        (positions[None, :] >= row_starts[:, None]) & (positions[None, :] < row_ends[:, None])
    ).astype(jnp.bfloat16)
    shard_ids = shard_of[0, :, 0]
    local_rows = jnp.arange(per_block, dtype=jnp.int32)
    earlier = (shard_ids[:, None] == shard_ids[None, :]) & (
        local_rows[None, :] < local_rows[:, None]
    )
    slot_rank = jnp.sum(earlier.astype(jnp.int32), 1)
    capacity = per_block // 2
    slot_ids = jnp.arange(capacity, dtype=jnp.int32)
    quarter = D // index_count
    summed = lax.psum_scatter(
        partial_value.astype(jnp.bfloat16), "index", scatter_dimension=1, tiled=True
    ).astype(jnp.float32)
    own_states = lax.dynamic_slice_in_dim(states, group_index * quarter, quarter, 1)
    layer = (own_states.astype(jnp.float32) + summed).astype(jnp.bfloat16)
    partial_pool = jnp.dot(member, layer, preferred_element_type=jnp.float32)
    pooled = lax.psum_scatter(
        partial_pool.astype(jnp.bfloat16), "seq", scatter_dimension=0, tiled=True
    ).astype(jnp.float32)
    shard_range = jnp.arange(index_count, dtype=jnp.int32)
    routing = (
        (shard_ids[None, None, :] == shard_range[:, None, None])
        & (slot_rank[None, None, :] == slot_ids[None, :, None])
    ).astype(jnp.float32)
    outgoing = jnp.einsum("rkc,cf->rkf", routing, pooled, precision=lax.Precision.HIGHEST)
    arrived = lax.all_to_all(outgoing, "index", split_axis=0, concat_axis=2, tiled=True)[0]
    shelf_rows = arrived * lax.rsqrt(jnp.mean(arrived * arrived, -1, keepdims=True) + 1e-06)
    return (layer[None], shelf_rows[None, None, None])


def lanes(shape):
    return lax.broadcasted_iota(jnp.int32, shape, 1)


def rotary(tile, cosine, sine):
    first = lanes(tile.shape) % HD < HD // 2
    partner = jnp.where(first, pltpu.roll(tile, 128 - HD // 2, 1), pltpu.roll(tile, HD // 2, 1))
    return tile * cosine + partner * sine


def attend_kernel(folded, pieces, *refs):
    where, h_refs, (cos_ref, sin_ref, member_ref) = refs[0], refs[1:5], refs[5:8]
    w_refs = refs[8 : 8 + pieces]
    out_refs = refs[8 + pieces : 12 + pieces]
    q_s, k_s, v_s, c_s = refs[12 + pieces :]
    s, d = where[0], where[1]
    rows = h_refs[0].shape[0]
    total = 4 * rows
    shard = h_refs[0].shape[1] // 4
    half = shard // 2

    for j in range(4):
        block = jnp.bitwise_xor(s, j)
        at = pl.ds(pl.multiple_of(block * rows, rows), rows)
        if folded:
            top = jnp.zeros((rows, 256), jnp.float32)
            bottom = jnp.zeros((rows, 256), jnp.float32)
            for k in range(4):
                column = lax.rem(d - k + 4, 4) * shard
                w = w_refs[k]
                h_top = h_refs[j][:, pl.ds(pl.multiple_of(column, half), half)]
                h_bottom = h_refs[j][:, pl.ds(pl.multiple_of(column + half, half), half)]
                top += jnp.dot(h_top, jnp.concatenate([w[:, 0:128], w[:, 256:384]], 1), preferred_element_type=jnp.float32)
                bottom += jnp.dot(h_bottom, w[:, 128:384], preferred_element_type=jnp.float32)
            qk = rotary(top[:, :128] + bottom[:, :128], cos_ref[at, :], sin_ref[at, :])
            low = lanes(qk.shape) < HD
            q_s[at, :] = jnp.where(low, qk * HD**-0.5, 0.0).astype(jnp.bfloat16)
            k_s[at, :] = pltpu.roll(qk, HD, 1).astype(jnp.bfloat16)
            v = top[:, 128:] + pltpu.roll(bottom[:, 128:], HD, 1)
            v_s[at, :] = jnp.where(low, v, 1.0).astype(jnp.bfloat16)
        else:
            acc = jnp.zeros((rows, 384), jnp.float32)
            for k in range(4):
                for p in range(2):
                    column = lax.rem(d - k + 4, 4) * shard + p * half
                    h_part = h_refs[j][:, pl.ds(pl.multiple_of(column, half), half)]
                    acc += jnp.dot(h_part, w_refs[2 * k + p][...], preferred_element_type=jnp.float32)
            q_s[at, :] = (rotary(acc[:, :128], cos_ref[at, :], sin_ref[at, :]) * HD**-0.5).astype(jnp.bfloat16)
            k_s[at, :] = rotary(acc[:, 128:256], cos_ref[at, :], sin_ref[at, :]).astype(jnp.bfloat16)
            v_s[at, 0:128] = acc[:, 256:].astype(jnp.bfloat16)
            v_s[at, 128:256] = jnp.ones((rows, 128), jnp.bfloat16)

    step = 128
    for r in range(total // step):
        start, end = max(0, r * step - HALF_WIN), min(total, (r + 1) * step + HALF_WIN)
        q_tile = q_s[r * step : (r + 1) * step, :]
        k_tile = k_s[start:end, :]
        v_tile = v_s[start:end, :]
        ahead = lax.broadcasted_iota(jnp.int32, (step, step), 1) - lax.broadcasted_iota(jnp.int32, (step, step), 0)
        low = lanes(q_tile.shape) < HD
        heads = []
        for head in range(1 if folded else 2):
            q = q_tile if folded else jnp.where(low if head == 0 else ~low, q_tile, jnp.zeros_like(q_tile))
            scores = lax.dot_general(q, k_tile, (((1,), (1,)), ((), ())), preferred_element_type=jnp.float32)
            parts = [scores]
            if start == r * step - HALF_WIN:
                parts = [jnp.where(ahead >= 0, scores[:, :step], -1e30), scores[:, step:]]
            if end == (r + 1) * step + HALF_WIN:
                last = parts.pop()
                parts += [last[:, :-step], jnp.where(ahead <= 0, last[:, -step:], -1e30)]
            scores = jnp.concatenate(parts, 1)
            expo = jnp.exp(scores - jnp.max(scores, 1, keepdims=True)).astype(jnp.bfloat16)
            o = jnp.dot(expo, v_tile, preferred_element_type=jnp.float32)
            if folded:
                heads.append(o / pltpu.roll(o, HD, 1))
            else:
                heads.append(o[:, :128] / o[:, 128:])
        context = heads[0] if folded else jnp.where(low, heads[0], heads[1])
        c_s[r * step : (r + 1) * step, :] = context.astype(jnp.bfloat16)

    pooled = jnp.dot(member_ref[...], c_s[...], preferred_element_type=jnp.float32)
    high = pooled.astype(jnp.bfloat16)
    rest = (pooled - high.astype(jnp.float32)).astype(jnp.bfloat16)
    per_block = pooled.shape[0] // 4
    for j in range(4):
        block = jnp.bitwise_xor(s, j)
        both = jnp.zeros((2 * per_block, 128), jnp.bfloat16)
        for b in range(4):
            cut = slice(b * per_block, (b + 1) * per_block)
            both = jnp.where(block == b, jnp.concatenate([high[cut], rest[cut]], 0), both)
        out = out_refs[j]
        if folded:
            lo = c_s[pl.ds(pl.multiple_of(block * rows, rows), rows // 2), :].astype(jnp.float32)
            hi = c_s[pl.ds(pl.multiple_of(block * rows + rows // 2, rows // 2), rows // 2), :].astype(jnp.float32)
            low = lanes(lo.shape) < HD
            out[0 : rows // 2, :] = jnp.where(low, lo, pltpu.roll(hi, HD, 1)).astype(jnp.bfloat16)
            out[rows // 2 :, :] = both
        else:
            out[0:rows, :] = c_s[pl.ds(pl.multiple_of(block * rows, rows), rows), :]
            out[rows:, :] = both


def attend(where, blocks, tables, pieces, folded):
    rows = blocks[0].shape[0]
    total = 4 * rows
    width = 128 if folded else 256
    out_rows = (rows // 2 if folded else rows) + 2 * tables[2].shape[0] // 4
    vmem = pl.BlockSpec(memory_space=pltpu.VMEM)
    return pl.pallas_call(
        functools.partial(attend_kernel, folded, len(pieces)),
        out_shape=[jax.ShapeDtypeStruct((out_rows, 128), jnp.bfloat16)] * 4,
        in_specs=[pl.BlockSpec(memory_space=pltpu.SMEM)] + [vmem] * (7 + len(pieces)),
        out_specs=[vmem] * 4,
        scratch_shapes=[
            pltpu.VMEM((total, 128), jnp.bfloat16),
            pltpu.VMEM((total, 128), jnp.bfloat16),
            pltpu.VMEM((total, width), jnp.bfloat16),
            pltpu.VMEM((total, 128), jnp.bfloat16),
        ],
        compiler_params=pltpu.CompilerParams(vmem_limit_bytes=40 * 2**20),
        name="attend_folded" if folded else "attend_tile",
    )(where, *blocks, *tables, *pieces)


def project_kernel(where, h_ref, pool_ref, route_ref, *refs):
    a_refs, b_refs, w_refs = refs[0:5], refs[5:10], refs[10:16]
    layer_ref, keep_ref, send_ref, c_s, o_s = refs[16:]
    s, d, g = where[0], where[1], where[2]
    rows = h_ref.shape[0]
    extra = a_refs[0].shape[0] - rows
    width = c_s.shape[1] // 2
    other = 1 - g
    odd = jnp.bitwise_and(s, 1) == 1
    group_of = (g, other)

    for t in range(2):
        base = group_of[t] * width
        a_parts = [r[...] for r in a_refs[0:4]] if t == 0 else [a_refs[4][j] for j in range(4)]
        b_parts = [r[...] for r in b_refs[0:4]] if t == 0 else [b_refs[4][j] for j in range(4)]
        for j in range(4):
            tile = jnp.bitwise_xor(s, j)
            c_s[:, pl.ds(pl.multiple_of(base + tile * 128, 128), 128)] = a_parts[j]
        for pair in range(2):
            tile = 4 + jnp.bitwise_xor(s // 2, pair)
            one, two = b_parts[2 * pair].astype(jnp.float32), b_parts[2 * pair + 1].astype(jnp.float32)
            left, right = jnp.where(odd, two, one), jnp.where(odd, one, two)
            low = lanes(left.shape) < HD
            first = jnp.where(low, left, pltpu.roll(right, HD, 1)).astype(jnp.bfloat16)
            second = jnp.where(low, pltpu.roll(left, HD, 1), right).astype(jnp.bfloat16)
            at = pl.ds(pl.multiple_of(base + tile * 128, 128), 128)
            c_s[0 : rows // 2, at] = first[0 : rows // 2]
            c_s[rows // 2 : rows, at] = second[0 : rows // 2]
            c_s[rows:, at] = first[rows // 2 :]

    feats = w_refs[0].shape[1]
    per_shard = 4 * feats
    for p in range(2):
        shard = lax.rem(d - p + 4, 4)
        in_half = lax.rem(shard, 2)
        for j in range(4):
            source = (w_refs[p], w_refs[4 + p], w_refs[2 + p], w_refs[4 + p])[j]
            quarter = jnp.bitwise_xor(s, j)
            total = jnp.zeros((rows + extra, feats), jnp.float32)
            for t in range(2):
                if j == 0 or j == 2:
                    w = source[t]
                else:
                    w = source[2 * (j // 2) + t]
                c = c_s[:, pl.ds(pl.multiple_of(group_of[t] * width, 128), width)]
                total += lax.dot_general(c, w, (((1,), (1,)), ((), ())), preferred_element_type=jnp.float32)
            column = pl.multiple_of(in_half * per_shard + quarter * feats, 128)
            o_s[:, pl.ds(column, feats)] = total[rows:]
            mine = h_ref[:, pl.ds(pl.multiple_of(g * 2 * per_shard + column, 128), feats)]
            layer_ref[:, pl.ds(column, feats)] = (mine.astype(jnp.float32) + total[:rows]).astype(jnp.bfloat16)

    half = extra // 2
    pooled = pool_ref[...] + o_s[0:half] + o_s[half:]
    routed = jnp.dot(route_ref[...], pooled, precision=lax.Precision.HIGHEST, preferred_element_type=jnp.float32)
    cut = routed.shape[0] // 2
    keep_ref[...] = jnp.where(g == 0, routed[:cut], routed[cut:])
    send_ref[...] = jnp.where(g == 0, routed[cut:], routed[:cut])


def project(where, h, pool, route, a_parts, b_parts, w_parts):
    rows, d_model = h.shape
    feats = d_model // 2
    extra = a_parts[0].shape[0] - rows
    vmem = pl.BlockSpec(memory_space=pltpu.VMEM)
    slots = route.shape[0] // 2
    return pl.pallas_call(
        project_kernel,
        out_shape=[
            jax.ShapeDtypeStruct((rows, feats), jnp.bfloat16),
            jax.ShapeDtypeStruct((slots, feats), jnp.float32),
            jax.ShapeDtypeStruct((slots, feats), jnp.float32),
        ],
        in_specs=[pl.BlockSpec(memory_space=pltpu.SMEM)] + [vmem] * 19,
        out_specs=[vmem] * 3,
        scratch_shapes=[
            pltpu.VMEM((rows + extra, 2 * w_parts[0].shape[2]), jnp.bfloat16),
            pltpu.VMEM((extra, feats), jnp.float32),
        ],
        compiler_params=pltpu.CompilerParams(vmem_limit_bytes=40 * 2**20),
        name="project",
    )(where, h, pool, route, *a_parts, *b_parts, *w_parts)


def xor_send(value, axis, j):
    return lax.ppermute(value, axis, [(i, i ^ j) for i in range(lax.axis_size(axis))])


def ring_send(value):
    count = lax.axis_size("dp")
    return lax.ppermute(value, "dp", [(i, (i + 1) % count) for i in range(count)])


def after(value, *earlier):
    return lax.optimization_barrier((value, *earlier))[0]


def body_by_heads(hidden, proj_weight, stretch_lengths, shard_of):
    h = hidden[0]
    rows = h.shape[0]
    shard = proj_weight.shape[1]
    s, d, g = lax.axis_index("seq"), lax.axis_index("dp"), lax.axis_index("index")
    where = jnp.stack([s, d, g]).astype(jnp.int32)
    total = 4 * rows

    mine = lax.dynamic_slice_in_dim(proj_weight[:3], s * 128, 128, 2)
    tile = jnp.concatenate([mine[0], mine[1], mine[2]], 1)
    a_ring = [[tile[: shard // 2], tile[shard // 2 :]]]
    pair = lax.dynamic_slice_in_dim(proj_weight[:3], (4 + s // 2) * 128, 128, 2)
    one = jnp.where(s % 2 == 1, pair[:, :, HD:], pair[:, :, :HD])
    top, bottom = one[:, : shard // 2], one[:, shard // 2 :]
    b_ring = [jnp.concatenate([top[0], top[1], bottom[0], bottom[1], top[2], bottom[2]], 1)]
    o_ring = [lax.dynamic_slice_in_dim(proj_weight[3], s * (shard // 4), shard // 4, 0)]

    h_cross = xor_send(h, "seq", 2)
    h_core = xor_send(h, "seq", 1)

    for step in range(3):
        a_ring.append([ring_send(a_ring[-1][0]), ring_send(a_ring[-1][1])])
    h_far = xor_send(h_cross, "seq", 1)
    blocks = [h, h_core, h_cross, h_far]

    for step in range(3):
        o_ring.append(ring_send(o_ring[-1]))
        b_ring.append(ring_send(b_ring[-1]))

    freqs = 10000.0 ** (-2.0 * jnp.arange(HD // 2, dtype=jnp.float32) / HD)
    angles = jnp.arange(total, dtype=jnp.float32)[:, None] * freqs[None, :]
    cosine, sine = jnp.cos(angles), jnp.sin(angles)
    cos_table = jnp.concatenate([cosine] * 4, 1)
    sin_table = jnp.concatenate([-sine, sine] * 2, 1)
    lengths = stretch_lengths[0]
    count = lengths.shape[0]
    per_block = count // 4
    ends = jnp.cumsum(lengths, dtype=jnp.int32)
    row_ids = jnp.arange(count, dtype=jnp.int32)
    order = row_ids % per_block * 4 + row_ids // per_block
    row_ends = ends[order]
    row_starts = row_ends - lengths[order]
    positions = jnp.arange(total, dtype=jnp.int32)
    member = (positions[None, :] >= row_starts[:, None]) & (positions[None, :] < row_ends[:, None])
    member = member.astype(jnp.bfloat16)
    tables = (cos_table, sin_table, member)

    own_member = lax.dynamic_slice_in_dim(member, s * per_block, per_block, 0)
    feats = h.shape[1] // 2
    pool = jnp.zeros((per_block, feats), jnp.float32)
    for j in range(4):
        part = lax.dynamic_slice_in_dim(blocks[j], g * feats, feats, 1)
        rows_of = lax.dynamic_slice_in_dim(own_member, (s ^ j) * rows, rows, 1)
        pool += jnp.dot(rows_of, part, preferred_element_type=jnp.float32)

    shard_ids = shard_of[0, :, 0]
    local = jnp.arange(per_block, dtype=jnp.int32)
    earlier = (shard_ids[:, None] == shard_ids[None, :]) & (local[None, :] < local[:, None])
    rank = jnp.sum(earlier.astype(jnp.int32), 1)
    capacity = per_block // 2
    slot = jnp.arange(2 * capacity, dtype=jnp.int32)
    route = (shard_ids * capacity + rank)[None, :] == slot[:, None]
    route = route.astype(jnp.float32)

    a_out = attend(where, blocks, tables, [piece for step in a_ring for piece in step], False)
    a_parts = [a_out[0]] + [xor_send(a_out[j], "seq", j) for j in (1, 2, 3)]
    a_parts.append(xor_send(jnp.stack(a_parts), "index", 1))

    own, cross, near = [], [], []
    for p in range(2):
        first_mine = (d - p) % 4 // 2 == g
        keep = jnp.where(first_mine, o_ring[p], o_ring[p + 2])
        send = jnp.where(first_mine, o_ring[p + 2], o_ring[p])
        both = jnp.stack([keep, xor_send(send, "index", 1)])
        over = xor_send(both, "seq", 2)
        own.append(both)
        cross.append(over)
        near.append(xor_send(jnp.concatenate([both, over]), "seq", 1))

    b_out = attend(where, blocks, tables, b_ring, True)
    b_parts = [b_out[0]] + [xor_send(b_out[j], "seq", j) for j in (1, 2, 3)]
    b_parts.append(xor_send(jnp.stack(b_parts), "index", 1))

    layer, keep, send = project(where, h, pool, route, a_parts, b_parts, own + cross + near)
    arrived = xor_send(send, "index", 1)
    square = (jnp.sum(keep * keep, -1, keepdims=True) + jnp.sum(arrived * arrived, -1, keepdims=True)) / (2 * feats)
    scale = lax.rsqrt(square + 1e-06)
    shelf = jnp.concatenate([jnp.where(g == 0, keep, arrived), jnp.where(g == 0, arrived, keep)], 1) * scale
    return (layer[None], shelf[None, None, None])


def solution(mesh):
    in_specs = (P("dp", "seq", None), P(None, "dp", "index"), P("dp", None), P("dp", "seq", None))
    out_specs = (P("dp", "seq", "index"), P("dp", "seq", "index", None, None))

    def whole(hidden, proj_weight, stretch_lengths, shard_of):
        heads = proj_weight.shape[2] // HD // mesh.shape["index"]
        rows = hidden.shape[1] // mesh.shape["seq"]
        by_heads = (mesh.shape["dp"], mesh.shape["seq"], mesh.shape["index"], heads, rows) == (4, 4, 2, 12, 256)
        return jax.shard_map(
            body_by_heads if by_heads else body,
            mesh=mesh,
            in_specs=in_specs,
            out_specs=out_specs,
            check_vma=False,
        )(hidden, proj_weight, stretch_lengths, shard_of)

    return whole
```

```python
import functools

import jax
import jax.numpy as jnp
import numpy as np
from jax import lax
from jax.experimental import pallas as pl
from jax.experimental.pallas import tpu as pltpu
from jax.sharding import PartitionSpec as P

D = 2048
HD = 64
HALF_WIN = 256

ATTEND = pl.CostEstimate(flops=4 * 10**9, bytes_accessed=1, transcendentals=0)
SHORT = pl.CostEstimate(flops=1, bytes_accessed=1, transcendentals=0)


def with_halo(cells, sides, width):
    for axis, dim in sides:
        count = lax.axis_size(axis)
        ends = count - 1
        head = lax.slice_in_dim(cells, 0, width, axis=dim)
        tail = lax.slice_in_dim(cells, cells.shape[dim] - width, cells.shape[dim], axis=dim)
        cells = jnp.concatenate(
            [
                lax.ppermute(tail, axis, [(i, (i + 1) % count) for i in range(ends)]),
                cells,
                lax.ppermute(head, axis, [((i + 1) % count, i) for i in range(ends)]),
            ],
            axis=dim,
        )
    return cells


def rotate(values_in, positions):
    half_dim = HD // 2
    freqs = 10000.0 ** (-2.0 * jnp.arange(half_dim, dtype=jnp.float32) / HD)
    angles = positions.astype(jnp.float32)[:, None] * freqs[None, :]
    cosine = jnp.cos(angles)[:, None, :]
    sine = jnp.sin(angles)[:, None, :]
    first = values_in[..., :half_dim]
    second = values_in[..., half_dim:]
    return jnp.concatenate([first * cosine - second * sine, second * cosine + first * sine], -1)


def window_heads(queries, key_rows, value_rows, visible):
    scale = HD ** (-0.5)

    def one_head(items):
        query_head, key_head, value_head = items
        scores = jnp.dot(query_head, key_head.T, preferred_element_type=jnp.float32) * scale
        scores = jnp.where(visible, scores, -1e30)
        maxima = jnp.max(scores, -1, keepdims=True)
        expo = jnp.exp(scores - maxima)
        weights = (expo / jnp.sum(expo, -1, keepdims=True)).astype(jnp.bfloat16)
        return jnp.dot(weights, value_head, preferred_element_type=jnp.float32).astype(jnp.bfloat16)

    context = lax.map(
        one_head,
        (jnp.moveaxis(queries, 1, 0), jnp.moveaxis(key_rows, 1, 0), jnp.moveaxis(value_rows, 1, 0)),
    )
    return jnp.moveaxis(context, 0, 1)


def body(hidden, proj_weight, stretch_lengths, shard_of):
    states = hidden[0]
    tokens_here = states.shape[0]
    width = proj_weight.shape[2]
    heads_here = width // HD
    seq_index = lax.axis_index("seq")
    group_index = lax.axis_index("index")
    seq_count = lax.axis_size("seq")
    index_count = lax.axis_size("index")
    total_length = tokens_here * seq_count
    positions = seq_index * tokens_here + jnp.arange(tokens_here, dtype=jnp.int32)
    projected = jnp.einsum(
        "td,jdc->jtc",
        states,
        lax.all_gather(proj_weight[:3], "dp", axis=1, tiled=True),
        preferred_element_type=jnp.float32,
    )
    queries = rotate(projected[0].reshape(tokens_here, heads_here, HD), positions).astype(
        jnp.bfloat16
    )
    key_rows = rotate(projected[1].reshape(tokens_here, heads_here, HD), positions).astype(
        jnp.bfloat16
    )
    value_rows = projected[2].astype(jnp.bfloat16)
    stacked = jnp.stack([key_rows.reshape(tokens_here, width), value_rows])
    padded = with_halo(stacked, (("seq", 1),), HALF_WIN)
    span = tokens_here + 2 * HALF_WIN
    key_part = padded[0, 0:span].reshape(span, heads_here, HD)
    value_part = padded[1, 0:span].reshape(span, heads_here, HD)
    key_pos = seq_index * tokens_here + 0 - HALF_WIN + jnp.arange(span, dtype=jnp.int32)
    visible = (
        (jnp.abs(key_pos[None, :] - positions[:, None]) <= HALF_WIN)
        & (key_pos[None, :] >= 0)
        & (key_pos[None, :] < total_length)
    )
    context_parts = window_heads(queries, key_part, value_part, visible).reshape(tokens_here, width)
    partial_value = lax.dot_general(
        context_parts,
        lax.all_gather(proj_weight[3], "dp", axis=0, tiled=True),
        (((1,), (1,)), ((), ())),
        preferred_element_type=jnp.float32,
    )
    lengths = stretch_lengths[0]
    stretch_count = lengths.shape[0]
    per_block = stretch_count // seq_count
    ends = jnp.cumsum(lengths, dtype=jnp.int32)
    starts = ends - lengths
    row_ids = jnp.arange(stretch_count, dtype=jnp.int32)
    order = row_ids % per_block * seq_count + row_ids // per_block
    row_starts = starts[order]
    row_ends = ends[order]
    member = (
        (positions[None, :] >= row_starts[:, None]) & (positions[None, :] < row_ends[:, None])
    ).astype(jnp.bfloat16)
    shard_ids = shard_of[0, :, 0]
    local_rows = jnp.arange(per_block, dtype=jnp.int32)
    earlier = (shard_ids[:, None] == shard_ids[None, :]) & (
        local_rows[None, :] < local_rows[:, None]
    )
    slot_rank = jnp.sum(earlier.astype(jnp.int32), 1)
    capacity = per_block // 2
    slot_ids = jnp.arange(capacity, dtype=jnp.int32)
    quarter = D // index_count
    summed = lax.psum_scatter(
        partial_value.astype(jnp.bfloat16), "index", scatter_dimension=1, tiled=True
    ).astype(jnp.float32)
    own_states = lax.dynamic_slice_in_dim(states, group_index * quarter, quarter, 1)
    layer = (own_states.astype(jnp.float32) + summed).astype(jnp.bfloat16)
    partial_pool = jnp.dot(member, layer, preferred_element_type=jnp.float32)
    pooled = lax.psum_scatter(
        partial_pool.astype(jnp.bfloat16), "seq", scatter_dimension=0, tiled=True
    ).astype(jnp.float32)
    shard_range = jnp.arange(index_count, dtype=jnp.int32)
    routing = (
        (shard_ids[None, None, :] == shard_range[:, None, None])
        & (slot_rank[None, None, :] == slot_ids[None, :, None])
    ).astype(jnp.float32)
    outgoing = jnp.einsum("rkc,cf->rkf", routing, pooled, precision=lax.Precision.HIGHEST)
    arrived = lax.all_to_all(outgoing, "index", split_axis=0, concat_axis=2, tiled=True)[0]
    shelf_rows = arrived * lax.rsqrt(jnp.mean(arrived * arrived, -1, keepdims=True) + 1e-06)
    return (layer[None], shelf_rows[None, None, None])


def lanes(shape):
    return lax.broadcasted_iota(jnp.int32, shape, 1)


def rotary(tile, cosine, sine):
    first = lanes(tile.shape) % HD < HD // 2
    partner = jnp.where(first, pltpu.roll(tile, 128 - HD // 2, 1), pltpu.roll(tile, HD // 2, 1))
    return tile * cosine + partner * sine


def folded(columns, odd):
    half = columns[0].shape[0] // 2
    low = lanes((half, 128)) < HD
    turn = lambda x: pltpu.roll(x, HD, 1)
    q, k, v = [[c[:half].astype(jnp.float32), c[half:].astype(jnp.float32)] for c in columns]
    parts = [jnp.where(low, jnp.where(odd, turn(q[p]), q[p]), jnp.where(odd, k[p], turn(k[p]))) for p in range(2)]
    parts.append(jnp.where(low, jnp.where(odd, turn(v[0]), v[0]), jnp.where(odd, v[1], turn(v[1]))))
    return jnp.concatenate(parts, 1).astype(columns[0].dtype)


def pieces_kernel(where, w_ref, x_ref, o_ref, out_ref, first_ref, second_ref, third_ref):
    out_ref[...] = o_ref[0]
    first_ref[...] = folded([w_ref[j] for j in range(3)], False)
    second_ref[...] = folded([w_ref[j] for j in range(3)], True)
    third_ref[...] = folded([x_ref[j] for j in range(3)], lax.rem(where[0], 2) == 1)


def pieces(where, proj_weight):
    _, shard, width = proj_weight.shape
    quarter = shard // 4
    return pl.pallas_call(
        pieces_kernel,
        grid_spec=pltpu.PrefetchScalarGridSpec(
            num_scalar_prefetch=1,
            grid=(1,),
            in_specs=[
                pl.BlockSpec((3, shard, 128), lambda i, where: (0, 0, where[0])),
                pl.BlockSpec((3, shard, 128), lambda i, where: (0, 0, 4 + where[0] // 2)),
                pl.BlockSpec((1, quarter, width), lambda i, where: (3, where[0], 0)),
            ],
            out_specs=[pl.BlockSpec((quarter, width), lambda i, where: (0, 0))]
            + [pl.BlockSpec((shard // 2, 384), lambda i, where: (0, 0))] * 3,
        ),
        out_shape=[jax.ShapeDtypeStruct((quarter, width), proj_weight.dtype)]
        + [jax.ShapeDtypeStruct((shard // 2, 384), proj_weight.dtype)] * 3,
        cost_estimate=SHORT,
        name="pieces",
    )(where, proj_weight, proj_weight, proj_weight)


def after(value, *earlier):
    return lax.optimization_barrier((value, *earlier))[0]


def members(lengths, positions):
    count = lengths.shape[1]
    shape = (count, count)
    row, other = lax.broadcasted_iota(jnp.int32, shape, 0), lax.broadcasted_iota(jnp.int32, shape, 1)
    per_block = count // 4
    stretch = lax.rem(row, per_block) * 4 + row // per_block
    values = jnp.broadcast_to(lengths, shape)
    ends = jnp.sum(jnp.where(other <= stretch, values, 0), 1, keepdims=True)
    starts = jnp.sum(jnp.where(other < stretch, values, 0), 1, keepdims=True)
    position = lax.broadcasted_iota(jnp.int32, (count, positions), 1)
    return jnp.where((position >= starts) & (position < ends), 1.0, 0.0).astype(jnp.bfloat16)


def attend_kernel(pools, *refs):
    where, h_refs, (cos_ref, sin_ref, lengths_ref), w_refs = refs[0], refs[1:5], refs[5:8], refs[8:12]
    out_refs = refs[12:16]
    q_s, k_s, v_s, c_s, member_s = refs[-5:]
    s, d, g = where[0], where[1], where[2]
    rows, d_model = h_refs[0].shape
    total = 4 * rows
    shard = d_model // 4
    half = shard // 2
    per_block = lengths_ref.shape[1] // 4
    member_s[...] = members(lengths_ref[...], total)

    for j in range(4):
        block = jnp.bitwise_xor(s, j)
        at = pl.ds(pl.multiple_of(block * rows, rows), rows)
        top = jnp.zeros((rows, 256), jnp.float32)
        bottom = jnp.zeros((rows, 256), jnp.float32)
        for k in range(4):
            column = lax.rem(d - k + 4, 4) * shard
            w = w_refs[k]
            h_top = h_refs[j][:, pl.ds(pl.multiple_of(column, half), half)]
            h_bottom = h_refs[j][:, pl.ds(pl.multiple_of(column + half, half), half)]
            top += jnp.dot(h_top, jnp.concatenate([w[:, 0:128], w[:, 256:384]], 1), preferred_element_type=jnp.float32)
            bottom += jnp.dot(h_bottom, w[:, 128:384], preferred_element_type=jnp.float32)
        qk = rotary(top[:, :128] + bottom[:, :128], cos_ref[at, :], sin_ref[at, :])
        low = lanes(qk.shape) < HD
        q_s[at, :] = jnp.where(low, qk * HD**-0.5, 0.0).astype(jnp.bfloat16)
        k_s[at, :] = pltpu.roll(qk, HD, 1).astype(jnp.bfloat16)
        v = top[:, 128:] + pltpu.roll(bottom[:, 128:], HD, 1)
        v_s[at, :] = jnp.where(low, v, 1.0).astype(jnp.bfloat16)

    step = 128
    for r in range(total // step):
        start, end = max(0, r * step - HALF_WIN), min(total, (r + 1) * step + HALF_WIN)
        ahead = lax.broadcasted_iota(jnp.int32, (step, step), 1) - lax.broadcasted_iota(jnp.int32, (step, step), 0)
        scores = lax.dot_general(
            q_s[r * step : (r + 1) * step, :], k_s[start:end, :], (((1,), (1,)), ((), ())), preferred_element_type=jnp.float32
        )
        parts = [scores]
        if start == r * step - HALF_WIN:
            parts = [jnp.where(ahead >= 0, scores[:, :step], -1e30), scores[:, step:]]
        if end == (r + 1) * step + HALF_WIN:
            last = parts.pop()
            parts += [last[:, :-step], jnp.where(ahead <= 0, last[:, -step:], -1e30)]
        scores = jnp.concatenate(parts, 1)
        expo = jnp.exp(scores - jnp.max(scores, 1, keepdims=True)).astype(jnp.bfloat16)
        o = jnp.dot(expo, v_s[start:end, :], preferred_element_type=jnp.float32)
        low = lanes(o.shape) < HD
        c_s[r * step : (r + 1) * step, :] = jnp.where(low, o / pltpu.roll(o, HD, 1), 0.0).astype(jnp.bfloat16)

    pooled = jnp.dot(member_s[...], c_s[...], preferred_element_type=jnp.float32)
    high = pooled.astype(jnp.bfloat16)
    rest = (pooled - high.astype(jnp.float32)).astype(jnp.bfloat16)
    for j in range(4):
        block = jnp.bitwise_xor(s, j)
        both = jnp.zeros((2 * per_block, 128), jnp.bfloat16)
        for b in range(4):
            cut = slice(b * per_block, (b + 1) * per_block)
            both = jnp.where(block == b, jnp.concatenate([high[cut], rest[cut]], 0), both)
        out = out_refs[j]
        lo = c_s[pl.ds(pl.multiple_of(block * rows, rows), rows // 2), :].astype(jnp.float32)
        hi = c_s[pl.ds(pl.multiple_of(block * rows + rows // 2, rows // 2), rows // 2), :].astype(jnp.float32)
        out[0 : rows // 2, :] = (lo + pltpu.roll(hi, HD, 1)).astype(jnp.bfloat16)
        out[rows // 2 :, :] = both

    if pools:
        feats = d_model // 2
        sums = jnp.zeros((4 * per_block, feats), jnp.float32)
        for j in range(4):
            rows_of = member_s[:, pl.ds(pl.multiple_of(jnp.bitwise_xor(s, j) * rows, rows), rows)]
            part = h_refs[j][:, pl.ds(pl.multiple_of(g * feats, feats), feats)]
            sums += jnp.dot(rows_of, part, preferred_element_type=jnp.float32)
        own = jnp.zeros((per_block, feats), jnp.float32)
        for b in range(4):
            own = jnp.where(s == b, sums[b * per_block : (b + 1) * per_block], own)
        refs[16][...] = own


def attend(where, blocks, tables, pieces, pools):
    rows, d_model = blocks[0].shape
    total = 4 * rows
    count = tables[2].shape[1]
    per_block = count // 4
    vmem = pl.BlockSpec(memory_space=pltpu.VMEM)
    out_shape = [jax.ShapeDtypeStruct((rows // 2 + 2 * per_block, 128), jnp.bfloat16)] * 4
    if pools:
        out_shape.append(jax.ShapeDtypeStruct((per_block, d_model // 2), jnp.float32))
    return pl.pallas_call(
        functools.partial(attend_kernel, pools),
        out_shape=out_shape,
        in_specs=[pl.BlockSpec(memory_space=pltpu.SMEM)] + [vmem] * 11,
        out_specs=[vmem] * len(out_shape),
        scratch_shapes=[pltpu.VMEM((total, 128), jnp.bfloat16)] * 4 + [pltpu.VMEM((count, total), jnp.bfloat16)],
        compiler_params=pltpu.CompilerParams(vmem_limit_bytes=24 * 2**20),
        cost_estimate=ATTEND,
        name="attend_and_pool" if pools else "attend",
    )(where, *blocks, *tables, *pieces)


def project_kernel(where, shard_ref, h_ref, pool_ref, *refs):
    heads = [refs[5 * i : 5 * i + 5] for i in range(3)]
    w_refs = refs[15:17]
    layer_ref, keep_ref, send_ref, c_s, o_s = refs[17:]
    s, d, g = where[0], where[1], where[2]
    rows = h_ref.shape[0]
    extra = c_s.shape[0] - rows
    width = c_s.shape[1] // 2
    odd = jnp.bitwise_and(s, 1) == 1
    group_of = (g, 1 - g)

    def place(base, tile, left, right):
        low = lanes(left.shape) < HD
        first = jnp.where(low, left, pltpu.roll(right, HD, 1)).astype(jnp.bfloat16)
        second = jnp.where(low, pltpu.roll(left, HD, 1), right).astype(jnp.bfloat16)
        at = pl.ds(pl.multiple_of(base + tile * 128, 128), 128)
        c_s[0 : rows // 2, at] = first[0 : rows // 2]
        c_s[rows // 2 : rows, at] = second[0 : rows // 2]
        c_s[rows:, at] = first[rows // 2 :]

    for t in range(2):
        base = group_of[t] * width
        parts = [[(r[j][...] if t == 0 else r[4][j]).astype(jnp.float32) for j in range(4)] for r in heads]
        for j in range(4):
            place(base, jnp.bitwise_xor(s, j), parts[0][j], parts[1][j])
        for pair in range(2):
            one, two = parts[2][2 * pair], parts[2][2 * pair + 1]
            left, right = jnp.where(odd, two, one), jnp.where(odd, one, two)
            place(base, 4 + jnp.bitwise_xor(s // 2, pair), left, right)

    feats = w_refs[0].shape[2]
    per_shard = 4 * feats
    for p in range(2):
        in_half = lax.rem(lax.rem(d - p + 4, 4), 2)
        for j in range(4):
            source = w_refs[j % 2]
            quarter = jnp.bitwise_xor(s, j)
            total = jnp.zeros((rows + extra, feats), jnp.float32)
            for t in range(2):
                w = source[2 * (j // 2) + t, p]
                c = c_s[:, pl.ds(pl.multiple_of(group_of[t] * width, 128), width)]
                total += lax.dot_general(c, w, (((1,), (1,)), ((), ())), preferred_element_type=jnp.float32)
            column = pl.multiple_of(in_half * per_shard + quarter * feats, 128)
            o_s[:, pl.ds(column, feats)] = total[rows:]
            mine = h_ref[:, pl.ds(pl.multiple_of(g * 2 * per_shard + column, 128), feats)]
            layer_ref[:, pl.ds(column, feats)] = (mine.astype(jnp.float32) + total[:rows]).astype(jnp.bfloat16)

    half = extra // 2
    pooled = pool_ref[...] + o_s[0:half] + o_s[half:]
    slots = 2 * keep_ref.shape[0]
    slot = lax.broadcasted_iota(jnp.int32, (slots, half), 0)
    source = lax.broadcasted_iota(jnp.int32, (slots, half), 1)
    route = jnp.zeros((slots, half), jnp.float32)
    ids = [shard_ref[c] for c in range(half)]
    for c in range(half):
        rank = sum([(ids[e] == ids[c]).astype(jnp.int32) for e in range(c)], jnp.int32(0))
        route = jnp.where((slot == ids[c] * (slots // 2) + rank) & (source == c), 1.0, route)
    routed = jnp.dot(route, pooled, precision=lax.Precision.HIGHEST, preferred_element_type=jnp.float32)
    cut = routed.shape[0] // 2
    keep_ref[...] = jnp.where(g == 0, routed[:cut], routed[cut:])
    send_ref[...] = jnp.where(g == 0, routed[cut:], routed[:cut])


def project(where, h, pool, shard_ids, contexts, w_parts):
    rows, d_model = h.shape
    feats = d_model // 2
    extra = contexts[0].shape[0] - rows // 2
    vmem = pl.BlockSpec(memory_space=pltpu.VMEM)
    slots = shard_ids.shape[0] // 2
    return pl.pallas_call(
        project_kernel,
        out_shape=[
            jax.ShapeDtypeStruct((rows, feats), jnp.bfloat16),
            jax.ShapeDtypeStruct((slots, feats), jnp.float32),
            jax.ShapeDtypeStruct((slots, feats), jnp.float32),
        ],
        in_specs=[pl.BlockSpec(memory_space=pltpu.SMEM)] * 2 + [vmem] * 19,
        out_specs=[vmem] * 3,
        scratch_shapes=[
            pltpu.VMEM((rows + extra, 2 * w_parts[0].shape[3]), jnp.bfloat16),
            pltpu.VMEM((extra, feats), jnp.float32),
        ],
        compiler_params=pltpu.CompilerParams(vmem_limit_bytes=24 * 2**20),
        cost_estimate=SHORT,
        name="project",
    )(where, shard_ids, h, pool, *contexts, *w_parts)


def xor_send(name, value, axis, j):
    with jax.named_scope(name):
        return lax.ppermute(value, axis, [(i, i ^ j) for i in range(lax.axis_size(axis))])


def ring_send(name, value):
    count = lax.axis_size("dp")
    with jax.named_scope(name):
        return lax.ppermute(value, "dp", [(i, (i + 1) % count) for i in range(count)])


def rotary_tables(total):
    freqs = np.float32(10000.0) ** (np.float32(-2.0) * np.arange(HD // 2, dtype=np.float32) / np.float32(HD))
    angles = (np.arange(total, dtype=np.float32)[:, None] * freqs[None, :]).astype(np.float64)
    cosine, sine = np.cos(angles).astype(np.float32), np.sin(angles).astype(np.float32)
    return jnp.asarray(np.concatenate([cosine] * 4, 1)), jnp.asarray(np.concatenate([-sine, sine] * 2, 1))


def body_by_heads(hidden, proj_weight, stretch_lengths, shard_of):
    h = hidden[0]
    rows = h.shape[0]
    s, d, g = lax.axis_index("seq"), lax.axis_index("dp"), lax.axis_index("index")
    where = jnp.stack([s, d, g]).astype(jnp.int32)
    total = 4 * rows

    tables = (*rotary_tables(total), stretch_lengths)

    def across(ring):
        pairs = [((d - p) % 4 // 2 == g, ring[p], ring[p + 2]) for p in range(2)]
        keep = jnp.stack([jnp.where(mine, one, two) for mine, one, two in pairs])
        send = jnp.stack([jnp.where(mine, two, one) for mine, one, two in pairs])
        with jax.named_scope("out_across"):
            far = lax.ppermute(send, ("seq", "index"), [(i, i ^ 5) for i in range(8)])
        return keep, xor_send("out_group", send, "index", 1), xor_send("out_cross", keep, "seq", 2), far

    def to_seq(name, parts):
        return [parts[0]] + [xor_send(name, parts[j], "seq", j) for j in (1, 2, 3)]

    def to_other(name, parts):
        return parts + [xor_send(name, jnp.stack(parts), "index", 1)]

    h_cross = xor_send("hidden_cross", h, "seq", 2)
    h_core = xor_send("hidden_core", h, "seq", 1)
    o0, x0, y0, z0 = pieces(where, proj_weight)

    def rings(names, starts):
        held = [[start] for start in starts]
        for step in range(3):
            for ring, name in zip(held, names):
                ring.append(ring_send(name, ring[-1]))
        return held

    out_ring, first_ring = rings(("out", "first"), (o0, x0))
    out_ring[3], first_ring[3], h_core, h_cross, y0, z0 = lax.optimization_barrier(
        (out_ring[3], first_ring[3], h_core, h_cross, y0, z0)
    )

    second_ring, third_ring = rings(("second", "third"), (y0, z0))
    h_far = xor_send("hidden_far", h_cross, "seq", 1)
    blocks = [h, h_core, h_cross, h_far]
    four = across(out_ring)
    first_ring[3] = after(first_ring[3], second_ring[2], third_ring[2])
    first = attend(where, blocks, tables, first_ring, True)
    first_parts = to_seq("context_first", first[:4])
    second = attend(where, blocks, tables, second_ring, False)
    third_ring[3], four, first_parts, second = lax.optimization_barrier((third_ring[3], four, first_parts, second))

    four = jnp.stack(four)
    near = xor_send("out_core", four, "seq", 1)
    first_parts = to_other("context_first_group", first_parts)
    second_parts = to_seq("context_second", second)
    third = attend(where, blocks, tables, third_ring, False)
    second_parts = to_other("context_second_group", second_parts)
    third_parts = to_other("context_third_group", to_seq("context_third", third))

    contexts = first_parts + second_parts + third_parts
    layer, keep, send = project(where, h, first[4], shard_of[0, :, 0], contexts, [four, near])
    arrived = xor_send("embedding_half", send, "index", 1)
    feats = keep.shape[1]
    square = (jnp.sum(keep * keep, -1, keepdims=True) + jnp.sum(arrived * arrived, -1, keepdims=True)) / (2 * feats)
    scale = lax.rsqrt(square + 1e-06)
    shelf = jnp.concatenate([jnp.where(g == 0, keep, arrived), jnp.where(g == 0, arrived, keep)], 1) * scale
    return (layer[None], shelf[None, None, None])


def solution(mesh):
    in_specs = (P("dp", "seq", None), P(None, "dp", "index"), P("dp", None), P("dp", "seq", None))
    out_specs = (P("dp", "seq", "index"), P("dp", "seq", "index", None, None))

    def whole(hidden, proj_weight, stretch_lengths, shard_of):
        heads = proj_weight.shape[2] // HD // mesh.shape["index"]
        rows = hidden.shape[1] // mesh.shape["seq"]
        by_heads = (mesh.shape["dp"], mesh.shape["seq"], mesh.shape["index"], heads, rows) == (4, 4, 2, 12, 256)
        return jax.shard_map(
            body_by_heads if by_heads else body,
            mesh=mesh,
            in_specs=in_specs,
            out_specs=out_specs,
            check_vma=False,
        )(hidden, proj_weight, stretch_lengths, shard_of)

    return whole
```

```python
import functools

import jax
import jax.numpy as jnp
import numpy as np
from jax import lax
from jax.experimental import pallas as pl
from jax.experimental.pallas import tpu as pltpu
from jax.sharding import PartitionSpec as P

D = 2048
HD = 64
HALF_WIN = 256

SHORT = pl.CostEstimate(flops=1, bytes_accessed=1, transcendentals=0)


def with_halo(cells, sides, width):
    for axis, dim in sides:
        count = lax.axis_size(axis)
        ends = count - 1
        head = lax.slice_in_dim(cells, 0, width, axis=dim)
        tail = lax.slice_in_dim(cells, cells.shape[dim] - width, cells.shape[dim], axis=dim)
        cells = jnp.concatenate(
            [
                lax.ppermute(tail, axis, [(i, (i + 1) % count) for i in range(ends)]),
                cells,
                lax.ppermute(head, axis, [((i + 1) % count, i) for i in range(ends)]),
            ],
            axis=dim,
        )
    return cells


def rotate(values_in, positions):
    half_dim = HD // 2
    freqs = 10000.0 ** (-2.0 * jnp.arange(half_dim, dtype=jnp.float32) / HD)
    angles = positions.astype(jnp.float32)[:, None] * freqs[None, :]
    cosine = jnp.cos(angles)[:, None, :]
    sine = jnp.sin(angles)[:, None, :]
    first = values_in[..., :half_dim]
    second = values_in[..., half_dim:]
    return jnp.concatenate([first * cosine - second * sine, second * cosine + first * sine], -1)


def window_heads(queries, key_rows, value_rows, visible):
    scale = HD ** (-0.5)

    def one_head(items):
        query_head, key_head, value_head = items
        scores = jnp.dot(query_head, key_head.T, preferred_element_type=jnp.float32) * scale
        scores = jnp.where(visible, scores, -1e30)
        maxima = jnp.max(scores, -1, keepdims=True)
        expo = jnp.exp(scores - maxima)
        weights = (expo / jnp.sum(expo, -1, keepdims=True)).astype(jnp.bfloat16)
        return jnp.dot(weights, value_head, preferred_element_type=jnp.float32).astype(jnp.bfloat16)

    context = lax.map(
        one_head,
        (jnp.moveaxis(queries, 1, 0), jnp.moveaxis(key_rows, 1, 0), jnp.moveaxis(value_rows, 1, 0)),
    )
    return jnp.moveaxis(context, 0, 1)


def body(hidden, proj_weight, stretch_lengths, shard_of):
    states = hidden[0]
    tokens_here = states.shape[0]
    width = proj_weight.shape[2]
    heads_here = width // HD
    seq_index = lax.axis_index("seq")
    group_index = lax.axis_index("index")
    seq_count = lax.axis_size("seq")
    index_count = lax.axis_size("index")
    total_length = tokens_here * seq_count
    positions = seq_index * tokens_here + jnp.arange(tokens_here, dtype=jnp.int32)
    projected = jnp.einsum(
        "td,jdc->jtc",
        states,
        lax.all_gather(proj_weight[:3], "dp", axis=1, tiled=True),
        preferred_element_type=jnp.float32,
    )
    queries = rotate(projected[0].reshape(tokens_here, heads_here, HD), positions).astype(
        jnp.bfloat16
    )
    key_rows = rotate(projected[1].reshape(tokens_here, heads_here, HD), positions).astype(
        jnp.bfloat16
    )
    value_rows = projected[2].astype(jnp.bfloat16)
    stacked = jnp.stack([key_rows.reshape(tokens_here, width), value_rows])
    padded = with_halo(stacked, (("seq", 1),), HALF_WIN)
    span = tokens_here + 2 * HALF_WIN
    key_part = padded[0, 0:span].reshape(span, heads_here, HD)
    value_part = padded[1, 0:span].reshape(span, heads_here, HD)
    key_pos = seq_index * tokens_here + 0 - HALF_WIN + jnp.arange(span, dtype=jnp.int32)
    visible = (
        (jnp.abs(key_pos[None, :] - positions[:, None]) <= HALF_WIN)
        & (key_pos[None, :] >= 0)
        & (key_pos[None, :] < total_length)
    )
    context_parts = window_heads(queries, key_part, value_part, visible).reshape(tokens_here, width)
    partial_value = lax.dot_general(
        context_parts,
        lax.all_gather(proj_weight[3], "dp", axis=0, tiled=True),
        (((1,), (1,)), ((), ())),
        preferred_element_type=jnp.float32,
    )
    lengths = stretch_lengths[0]
    stretch_count = lengths.shape[0]
    per_block = stretch_count // seq_count
    ends = jnp.cumsum(lengths, dtype=jnp.int32)
    starts = ends - lengths
    row_ids = jnp.arange(stretch_count, dtype=jnp.int32)
    order = row_ids % per_block * seq_count + row_ids // per_block
    row_starts = starts[order]
    row_ends = ends[order]
    member = (
        (positions[None, :] >= row_starts[:, None]) & (positions[None, :] < row_ends[:, None])
    ).astype(jnp.bfloat16)
    shard_ids = shard_of[0, :, 0]
    local_rows = jnp.arange(per_block, dtype=jnp.int32)
    earlier = (shard_ids[:, None] == shard_ids[None, :]) & (
        local_rows[None, :] < local_rows[:, None]
    )
    slot_rank = jnp.sum(earlier.astype(jnp.int32), 1)
    capacity = per_block // 2
    slot_ids = jnp.arange(capacity, dtype=jnp.int32)
    quarter = D // index_count
    summed = lax.psum_scatter(
        partial_value.astype(jnp.bfloat16), "index", scatter_dimension=1, tiled=True
    ).astype(jnp.float32)
    own_states = lax.dynamic_slice_in_dim(states, group_index * quarter, quarter, 1)
    layer = (own_states.astype(jnp.float32) + summed).astype(jnp.bfloat16)
    partial_pool = jnp.dot(member, layer, preferred_element_type=jnp.float32)
    pooled = lax.psum_scatter(
        partial_pool.astype(jnp.bfloat16), "seq", scatter_dimension=0, tiled=True
    ).astype(jnp.float32)
    shard_range = jnp.arange(index_count, dtype=jnp.int32)
    routing = (
        (shard_ids[None, None, :] == shard_range[:, None, None])
        & (slot_rank[None, None, :] == slot_ids[None, :, None])
    ).astype(jnp.float32)
    outgoing = jnp.einsum("rkc,cf->rkf", routing, pooled, precision=lax.Precision.HIGHEST)
    arrived = lax.all_to_all(outgoing, "index", split_axis=0, concat_axis=2, tiled=True)[0]
    shelf_rows = arrived * lax.rsqrt(jnp.mean(arrived * arrived, -1, keepdims=True) + 1e-06)
    return (layer[None], shelf_rows[None, None, None])


def lanes(shape):
    return lax.broadcasted_iota(jnp.int32, shape, 1)


def rotary(tile, cosine, sine):
    first = lanes(tile.shape) % HD < HD // 2
    partner = jnp.where(first, pltpu.roll(tile, 128 - HD // 2, 1), pltpu.roll(tile, HD // 2, 1))
    return tile * cosine + partner * sine


def folded(columns, odd):
    half = columns[0].shape[0] // 2
    low = lanes((half, 128)) < HD
    turn = lambda x: pltpu.roll(x, HD, 1)
    q, k, v = [[c[:half].astype(jnp.float32), c[half:].astype(jnp.float32)] for c in columns]
    parts = [jnp.where(low, jnp.where(odd, turn(q[p]), q[p]), jnp.where(odd, k[p], turn(k[p]))) for p in range(2)]
    parts.append(jnp.where(low, jnp.where(odd, turn(v[0]), v[0]), jnp.where(odd, v[1], turn(v[1]))))
    return jnp.concatenate(parts, 1).astype(columns[0].dtype)


def pieces_kernel(where, w_ref, x_ref, o_ref, out_ref, first_ref, second_ref, third_ref):
    out_ref[...] = o_ref[0]
    first_ref[...] = folded([w_ref[j] for j in range(3)], False)
    second_ref[...] = folded([w_ref[j] for j in range(3)], True)
    third_ref[...] = folded([x_ref[j] for j in range(3)], lax.rem(where[0], 2) == 1)


def pieces(where, proj_weight):
    _, shard, width = proj_weight.shape
    quarter = shard // 4
    return pl.pallas_call(
        pieces_kernel,
        grid_spec=pltpu.PrefetchScalarGridSpec(
            num_scalar_prefetch=1,
            grid=(1,),
            in_specs=[
                pl.BlockSpec((3, shard, 128), lambda i, where: (0, 0, where[0])),
                pl.BlockSpec((3, shard, 128), lambda i, where: (0, 0, 4 + where[0] // 2)),
                pl.BlockSpec((1, quarter, width), lambda i, where: (3, where[0], 0)),
            ],
            out_specs=[pl.BlockSpec((quarter, width), lambda i, where: (0, 0))]
            + [pl.BlockSpec((shard // 2, 384), lambda i, where: (0, 0))] * 3,
        ),
        out_shape=[jax.ShapeDtypeStruct((quarter, width), proj_weight.dtype)]
        + [jax.ShapeDtypeStruct((shard // 2, 384), proj_weight.dtype)] * 3,
        cost_estimate=SHORT,
        name="pieces",
    )(where, proj_weight, proj_weight, proj_weight)


def after(value, *earlier):
    return lax.optimization_barrier((value, *earlier))[0]


def members(lengths, positions):
    count = lengths.shape[1]
    shape = (count, count)
    row, other = lax.broadcasted_iota(jnp.int32, shape, 0), lax.broadcasted_iota(jnp.int32, shape, 1)
    per_block = count // 4
    stretch = lax.rem(row, per_block) * 4 + row // per_block
    values = jnp.broadcast_to(lengths, shape)
    ends = jnp.sum(jnp.where(other <= stretch, values, 0), 1, keepdims=True)
    starts = jnp.sum(jnp.where(other < stretch, values, 0), 1, keepdims=True)
    position = lax.broadcasted_iota(jnp.int32, (count, positions), 1)
    return jnp.where((position >= starts) & (position < ends), 1.0, 0.0).astype(jnp.bfloat16)


def attend_kernel(pools, *refs):
    where, h_refs, (cos_ref, sin_ref, lengths_ref), w_refs = refs[0], refs[1:5], refs[5:8], refs[8:12]
    out_refs = refs[12:16]
    q_s, k_s, v_s, c_s, member_s = refs[-5:]
    s, d, g = where[0], where[1], where[2]
    rows, d_model = h_refs[0].shape
    total = 4 * rows
    shard = d_model // 4
    half = shard // 2
    per_block = lengths_ref.shape[1] // 4
    member_s[...] = members(lengths_ref[...], total)

    for j in range(4):
        block = jnp.bitwise_xor(s, j)
        at = pl.ds(pl.multiple_of(block * rows, rows), rows)
        top = jnp.zeros((rows, 256), jnp.float32)
        bottom = jnp.zeros((rows, 256), jnp.float32)
        for k in range(4):
            column = lax.rem(d - k + 4, 4) * shard
            w = w_refs[k]
            h_top = h_refs[j][:, pl.ds(pl.multiple_of(column, half), half)]
            h_bottom = h_refs[j][:, pl.ds(pl.multiple_of(column + half, half), half)]
            top += jnp.dot(h_top, jnp.concatenate([w[:, 0:128], w[:, 256:384]], 1), preferred_element_type=jnp.float32)
            bottom += jnp.dot(h_bottom, w[:, 128:384], preferred_element_type=jnp.float32)
        qk = rotary(top[:, :128] + bottom[:, :128], cos_ref[at, :], sin_ref[at, :])
        low = lanes(qk.shape) < HD
        q_s[at, :] = jnp.where(low, qk * HD**-0.5, 0.0).astype(jnp.bfloat16)
        k_s[at, :] = pltpu.roll(qk, HD, 1).astype(jnp.bfloat16)
        v = top[:, 128:] + pltpu.roll(bottom[:, 128:], HD, 1)
        v_s[at, :] = jnp.where(low, v, 1.0).astype(jnp.bfloat16)

    step = 128
    for r in range(total // step):
        start, end = max(0, r * step - HALF_WIN), min(total, (r + 1) * step + HALF_WIN)
        ahead = lax.broadcasted_iota(jnp.int32, (step, step), 1) - lax.broadcasted_iota(jnp.int32, (step, step), 0)
        scores = lax.dot_general(
            q_s[r * step : (r + 1) * step, :], k_s[start:end, :], (((1,), (1,)), ((), ())), preferred_element_type=jnp.float32
        )
        parts = [scores]
        if start == r * step - HALF_WIN:
            parts = [jnp.where(ahead >= 0, scores[:, :step], -1e30), scores[:, step:]]
        if end == (r + 1) * step + HALF_WIN:
            last = parts.pop()
            parts += [last[:, :-step], jnp.where(ahead <= 0, last[:, -step:], -1e30)]
        scores = jnp.concatenate(parts, 1)
        expo = jnp.exp(scores - jnp.max(scores, 1, keepdims=True)).astype(jnp.bfloat16)
        o = jnp.dot(expo, v_s[start:end, :], preferred_element_type=jnp.float32)
        low = lanes(o.shape) < HD
        c_s[r * step : (r + 1) * step, :] = jnp.where(low, o / pltpu.roll(o, HD, 1), 0.0).astype(jnp.bfloat16)

    pooled = jnp.dot(member_s[...], c_s[...], preferred_element_type=jnp.float32)
    high = pooled.astype(jnp.bfloat16)
    rest = (pooled - high.astype(jnp.float32)).astype(jnp.bfloat16)
    for j in range(4):
        block = jnp.bitwise_xor(s, j)
        both = jnp.zeros((2 * per_block, 128), jnp.bfloat16)
        for b in range(4):
            cut = slice(b * per_block, (b + 1) * per_block)
            both = jnp.where(block == b, jnp.concatenate([high[cut], rest[cut]], 0), both)
        out = out_refs[j]
        lo = c_s[pl.ds(pl.multiple_of(block * rows, rows), rows // 2), :].astype(jnp.float32)
        hi = c_s[pl.ds(pl.multiple_of(block * rows + rows // 2, rows // 2), rows // 2), :].astype(jnp.float32)
        out[0 : rows // 2, :] = (lo + pltpu.roll(hi, HD, 1)).astype(jnp.bfloat16)
        out[rows // 2 :, :] = both

    if pools:
        feats = d_model // 2
        sums = jnp.zeros((4 * per_block, feats), jnp.float32)
        for j in range(4):
            rows_of = member_s[:, pl.ds(pl.multiple_of(jnp.bitwise_xor(s, j) * rows, rows), rows)]
            part = h_refs[j][:, pl.ds(pl.multiple_of(g * feats, feats), feats)]
            sums += jnp.dot(rows_of, part, preferred_element_type=jnp.float32)
        own = jnp.zeros((per_block, feats), jnp.float32)
        for b in range(4):
            own = jnp.where(s == b, sums[b * per_block : (b + 1) * per_block], own)
        refs[16][...] = own


def attend(where, blocks, tables, pieces, pools):
    rows, d_model = blocks[0].shape
    total = 4 * rows
    count = tables[2].shape[1]
    per_block = count // 4
    vmem = pl.BlockSpec(memory_space=pltpu.VMEM)
    out_shape = [jax.ShapeDtypeStruct((rows // 2 + 2 * per_block, 128), jnp.bfloat16)] * 4
    if pools:
        out_shape.append(jax.ShapeDtypeStruct((per_block, d_model // 2), jnp.float32))
    return pl.pallas_call(
        functools.partial(attend_kernel, pools),
        out_shape=out_shape,
        in_specs=[pl.BlockSpec(memory_space=pltpu.SMEM)] + [vmem] * 11,
        out_specs=[vmem] * len(out_shape),
        scratch_shapes=[pltpu.VMEM((total, 128), jnp.bfloat16)] * 4 + [pltpu.VMEM((count, total), jnp.bfloat16)],
        compiler_params=pltpu.CompilerParams(vmem_limit_bytes=24 * 2**20),
        cost_estimate=SHORT,
        name="attend_and_pool" if pools else "attend",
    )(where, *blocks, *tables, *pieces)


def project_kernel(where, shard_ref, h_ref, pool_ref, *refs):
    heads = [refs[5 * i : 5 * i + 5] for i in range(3)]
    w_refs = refs[15:17]
    layer_ref, keep_ref, send_ref, c_s, o_s = refs[17:]
    s, d, g = where[0], where[1], where[2]
    rows = h_ref.shape[0]
    extra = c_s.shape[0] - rows
    width = c_s.shape[1] // 2
    odd = jnp.bitwise_and(s, 1) == 1
    group_of = (g, 1 - g)

    def place(base, tile, left, right):
        low = lanes(left.shape) < HD
        first = jnp.where(low, left, pltpu.roll(right, HD, 1)).astype(jnp.bfloat16)
        second = jnp.where(low, pltpu.roll(left, HD, 1), right).astype(jnp.bfloat16)
        at = pl.ds(pl.multiple_of(base + tile * 128, 128), 128)
        c_s[0 : rows // 2, at] = first[0 : rows // 2]
        c_s[rows // 2 : rows, at] = second[0 : rows // 2]
        c_s[rows:, at] = first[rows // 2 :]

    for t in range(2):
        base = group_of[t] * width
        parts = [[(r[j][...] if t == 0 else r[4][j]).astype(jnp.float32) for j in range(4)] for r in heads]
        for j in range(4):
            place(base, jnp.bitwise_xor(s, j), parts[0][j], parts[1][j])
        for pair in range(2):
            one, two = parts[2][2 * pair], parts[2][2 * pair + 1]
            left, right = jnp.where(odd, two, one), jnp.where(odd, one, two)
            place(base, 4 + jnp.bitwise_xor(s // 2, pair), left, right)

    feats = w_refs[0].shape[2]
    per_shard = 4 * feats
    for p in range(2):
        in_half = lax.rem(lax.rem(d - p + 4, 4), 2)
        for j in range(4):
            source = w_refs[j % 2]
            quarter = jnp.bitwise_xor(s, j)
            total = jnp.zeros((rows + extra, feats), jnp.float32)
            for t in range(2):
                w = source[2 * (j // 2) + t, p]
                c = c_s[:, pl.ds(pl.multiple_of(group_of[t] * width, 128), width)]
                total += lax.dot_general(c, w, (((1,), (1,)), ((), ())), preferred_element_type=jnp.float32)
            column = pl.multiple_of(in_half * per_shard + quarter * feats, 128)
            o_s[:, pl.ds(column, feats)] = total[rows:]
            mine = h_ref[:, pl.ds(pl.multiple_of(g * 2 * per_shard + column, 128), feats)]
            layer_ref[:, pl.ds(column, feats)] = (mine.astype(jnp.float32) + total[:rows]).astype(jnp.bfloat16)

    half = extra // 2
    pooled = pool_ref[...] + o_s[0:half] + o_s[half:]
    slots = 2 * keep_ref.shape[0]
    slot = lax.broadcasted_iota(jnp.int32, (slots, half), 0)
    source = lax.broadcasted_iota(jnp.int32, (slots, half), 1)
    route = jnp.zeros((slots, half), jnp.float32)
    ids = [shard_ref[c] for c in range(half)]
    for c in range(half):
        rank = sum([(ids[e] == ids[c]).astype(jnp.int32) for e in range(c)], jnp.int32(0))
        route = jnp.where((slot == ids[c] * (slots // 2) + rank) & (source == c), 1.0, route)
    routed = jnp.dot(route, pooled, precision=lax.Precision.HIGHEST, preferred_element_type=jnp.float32)
    cut = routed.shape[0] // 2
    keep_ref[...] = jnp.where(g == 0, routed[:cut], routed[cut:])
    send_ref[...] = jnp.where(g == 0, routed[cut:], routed[:cut])


def project(where, h, pool, shard_ids, contexts, w_parts):
    rows, d_model = h.shape
    feats = d_model // 2
    extra = contexts[0].shape[0] - rows // 2
    vmem = pl.BlockSpec(memory_space=pltpu.VMEM)
    slots = shard_ids.shape[0] // 2
    return pl.pallas_call(
        project_kernel,
        out_shape=[
            jax.ShapeDtypeStruct((rows, feats), jnp.bfloat16),
            jax.ShapeDtypeStruct((slots, feats), jnp.float32),
            jax.ShapeDtypeStruct((slots, feats), jnp.float32),
        ],
        in_specs=[pl.BlockSpec(memory_space=pltpu.SMEM)] * 2 + [vmem] * 19,
        out_specs=[vmem] * 3,
        scratch_shapes=[
            pltpu.VMEM((rows + extra, 2 * w_parts[0].shape[3]), jnp.bfloat16),
            pltpu.VMEM((extra, feats), jnp.float32),
        ],
        compiler_params=pltpu.CompilerParams(vmem_limit_bytes=24 * 2**20),
        cost_estimate=SHORT,
        name="project",
    )(where, shard_ids, h, pool, *contexts, *w_parts)


def xor_send(name, value, axis, j):
    with jax.named_scope(name):
        return lax.ppermute(value, axis, [(i, i ^ j) for i in range(lax.axis_size(axis))])


def ring_send(name, value):
    count = lax.axis_size("dp")
    with jax.named_scope(name):
        return lax.ppermute(value, "dp", [(i, (i + 1) % count) for i in range(count)])


def rotary_tables(total):
    freqs = np.float32(10000.0) ** (np.float32(-2.0) * np.arange(HD // 2, dtype=np.float32) / np.float32(HD))
    angles = (np.arange(total, dtype=np.float32)[:, None] * freqs[None, :]).astype(np.float64)
    cosine, sine = np.cos(angles).astype(np.float32), np.sin(angles).astype(np.float32)
    return jnp.asarray(np.concatenate([cosine] * 4, 1)), jnp.asarray(np.concatenate([-sine, sine] * 2, 1))


def body_by_heads(hidden, proj_weight, stretch_lengths, shard_of):
    h = hidden[0]
    rows = h.shape[0]
    s, d, g = lax.axis_index("seq"), lax.axis_index("dp"), lax.axis_index("index")
    where = jnp.stack([s, d, g]).astype(jnp.int32)
    total = 4 * rows

    tables = (*rotary_tables(total), stretch_lengths)

    def across(ring):
        pairs = [((d - p) % 4 // 2 == g, ring[p], ring[p + 2]) for p in range(2)]
        keep = jnp.stack([jnp.where(mine, one, two) for mine, one, two in pairs])
        send = jnp.stack([jnp.where(mine, two, one) for mine, one, two in pairs])
        with jax.named_scope("out_across"):
            far = lax.ppermute(send, ("seq", "index"), [(i, i ^ 5) for i in range(8)])
        return keep, xor_send("out_group", send, "index", 1), xor_send("out_cross", keep, "seq", 2), far

    def to_seq(name, parts):
        return [parts[0]] + [xor_send(name, parts[j], "seq", j) for j in (1, 2, 3)]

    def to_other(name, parts):
        return parts + [xor_send(name, jnp.stack(parts), "index", 1)]

    h_cross = xor_send("hidden_cross", h, "seq", 2)
    h_core = xor_send("hidden_core", h, "seq", 1)
    o0, x0, y0, z0 = pieces(where, proj_weight)

    def rings(names, starts, **before):
        held = [[start] for start in starts]
        for step in range(3):
            for ring, name in zip(held, names):
                ring.append(ring_send(name, after(ring[-1], before[name]) if step == 1 and name in before else ring[-1]))
        return held

    out_ring, first_ring = rings(("out", "first"), (o0, x0))
    out_ring[3], first_ring[3], h_core, h_cross, y0, z0 = lax.optimization_barrier(
        (out_ring[3], first_ring[3], h_core, h_cross, y0, z0)
    )

    h_far = xor_send("hidden_far", h_cross, "seq", 1)
    second_ring, third_ring = rings(("second", "third"), (y0, z0), third=h_far)
    blocks = [h, h_core, h_cross, h_far]
    four = across(out_ring)
    first_ring[3] = after(first_ring[3], second_ring[2], third_ring[2])
    first = attend(where, blocks, tables, first_ring, True)
    first_parts = to_seq("context_first", first[:4])
    second = attend(where, blocks, tables, second_ring, False)
    third_ring[3], four, first_parts, second = lax.optimization_barrier((third_ring[3], four, first_parts, second))

    four = jnp.stack(four)
    near = xor_send("out_core", four, "seq", 1)
    first_parts = to_other("context_first_group", first_parts)
    second_parts = to_seq("context_second", second)
    third = attend(where, blocks, tables, third_ring, False)
    second_parts = to_other("context_second_group", second_parts)
    third_parts = to_other("context_third_group", to_seq("context_third", third))

    contexts = first_parts + second_parts + third_parts
    layer, keep, send = project(where, h, first[4], shard_of[0, :, 0], contexts, [four, near])
    arrived = xor_send("embedding_half", send, "index", 1)
    feats = keep.shape[1]
    square = (jnp.sum(keep * keep, -1, keepdims=True) + jnp.sum(arrived * arrived, -1, keepdims=True)) / (2 * feats)
    scale = lax.rsqrt(square + 1e-06)
    shelf = jnp.concatenate([jnp.where(g == 0, keep, arrived), jnp.where(g == 0, arrived, keep)], 1) * scale
    return (layer[None], shelf[None, None, None])


def solution(mesh):
    in_specs = (P("dp", "seq", None), P(None, "dp", "index"), P("dp", None), P("dp", "seq", None))
    out_specs = (P("dp", "seq", "index"), P("dp", "seq", "index", None, None))

    def whole(hidden, proj_weight, stretch_lengths, shard_of):
        heads = proj_weight.shape[2] // HD // mesh.shape["index"]
        rows = hidden.shape[1] // mesh.shape["seq"]
        by_heads = (mesh.shape["dp"], mesh.shape["seq"], mesh.shape["index"], heads, rows) == (4, 4, 2, 12, 256)
        return jax.shard_map(
            body_by_heads if by_heads else body,
            mesh=mesh,
            in_specs=in_specs,
            out_specs=out_specs,
            check_vma=False,
        )(hidden, proj_weight, stretch_lengths, shard_of)

    return whole
```

```python
import functools

import jax
import jax.numpy as jnp
import numpy as np
from jax import lax
from jax.experimental import pallas as pl
from jax.experimental.pallas import tpu as pltpu
from jax.sharding import PartitionSpec as P

D = 2048
HD = 64
HALF_WIN = 256

SHORT = pl.CostEstimate(flops=1, bytes_accessed=1, transcendentals=0)


def with_halo(cells, sides, width):
    for axis, dim in sides:
        count = lax.axis_size(axis)
        ends = count - 1
        head = lax.slice_in_dim(cells, 0, width, axis=dim)
        tail = lax.slice_in_dim(cells, cells.shape[dim] - width, cells.shape[dim], axis=dim)
        cells = jnp.concatenate(
            [
                lax.ppermute(tail, axis, [(i, (i + 1) % count) for i in range(ends)]),
                cells,
                lax.ppermute(head, axis, [((i + 1) % count, i) for i in range(ends)]),
            ],
            axis=dim,
        )
    return cells


def rotate(values_in, positions):
    half_dim = HD // 2
    freqs = 10000.0 ** (-2.0 * jnp.arange(half_dim, dtype=jnp.float32) / HD)
    angles = positions.astype(jnp.float32)[:, None] * freqs[None, :]
    cosine = jnp.cos(angles)[:, None, :]
    sine = jnp.sin(angles)[:, None, :]
    first = values_in[..., :half_dim]
    second = values_in[..., half_dim:]
    return jnp.concatenate([first * cosine - second * sine, second * cosine + first * sine], -1)


def window_heads(queries, key_rows, value_rows, visible):
    scale = HD ** (-0.5)

    def one_head(items):
        query_head, key_head, value_head = items
        scores = jnp.dot(query_head, key_head.T, preferred_element_type=jnp.float32) * scale
        scores = jnp.where(visible, scores, -1e30)
        maxima = jnp.max(scores, -1, keepdims=True)
        expo = jnp.exp(scores - maxima)
        weights = (expo / jnp.sum(expo, -1, keepdims=True)).astype(jnp.bfloat16)
        return jnp.dot(weights, value_head, preferred_element_type=jnp.float32).astype(jnp.bfloat16)

    context = lax.map(
        one_head,
        (jnp.moveaxis(queries, 1, 0), jnp.moveaxis(key_rows, 1, 0), jnp.moveaxis(value_rows, 1, 0)),
    )
    return jnp.moveaxis(context, 0, 1)


def body(hidden, proj_weight, stretch_lengths, shard_of):
    states = hidden[0]
    tokens_here = states.shape[0]
    width = proj_weight.shape[2]
    heads_here = width // HD
    seq_index = lax.axis_index("seq")
    group_index = lax.axis_index("index")
    seq_count = lax.axis_size("seq")
    index_count = lax.axis_size("index")
    total_length = tokens_here * seq_count
    positions = seq_index * tokens_here + jnp.arange(tokens_here, dtype=jnp.int32)
    projected = jnp.einsum(
        "td,jdc->jtc",
        states,
        lax.all_gather(proj_weight[:3], "dp", axis=1, tiled=True),
        preferred_element_type=jnp.float32,
    )
    queries = rotate(projected[0].reshape(tokens_here, heads_here, HD), positions).astype(
        jnp.bfloat16
    )
    key_rows = rotate(projected[1].reshape(tokens_here, heads_here, HD), positions).astype(
        jnp.bfloat16
    )
    value_rows = projected[2].astype(jnp.bfloat16)
    stacked = jnp.stack([key_rows.reshape(tokens_here, width), value_rows])
    padded = with_halo(stacked, (("seq", 1),), HALF_WIN)
    span = tokens_here + 2 * HALF_WIN
    key_part = padded[0, 0:span].reshape(span, heads_here, HD)
    value_part = padded[1, 0:span].reshape(span, heads_here, HD)
    key_pos = seq_index * tokens_here + 0 - HALF_WIN + jnp.arange(span, dtype=jnp.int32)
    visible = (
        (jnp.abs(key_pos[None, :] - positions[:, None]) <= HALF_WIN)
        & (key_pos[None, :] >= 0)
        & (key_pos[None, :] < total_length)
    )
    context_parts = window_heads(queries, key_part, value_part, visible).reshape(tokens_here, width)
    partial_value = lax.dot_general(
        context_parts,
        lax.all_gather(proj_weight[3], "dp", axis=0, tiled=True),
        (((1,), (1,)), ((), ())),
        preferred_element_type=jnp.float32,
    )
    lengths = stretch_lengths[0]
    stretch_count = lengths.shape[0]
    per_block = stretch_count // seq_count
    ends = jnp.cumsum(lengths, dtype=jnp.int32)
    starts = ends - lengths
    row_ids = jnp.arange(stretch_count, dtype=jnp.int32)
    order = row_ids % per_block * seq_count + row_ids // per_block
    row_starts = starts[order]
    row_ends = ends[order]
    member = (
        (positions[None, :] >= row_starts[:, None]) & (positions[None, :] < row_ends[:, None])
    ).astype(jnp.bfloat16)
    shard_ids = shard_of[0, :, 0]
    local_rows = jnp.arange(per_block, dtype=jnp.int32)
    earlier = (shard_ids[:, None] == shard_ids[None, :]) & (
        local_rows[None, :] < local_rows[:, None]
    )
    slot_rank = jnp.sum(earlier.astype(jnp.int32), 1)
    capacity = per_block // 2
    slot_ids = jnp.arange(capacity, dtype=jnp.int32)
    quarter = D // index_count
    summed = lax.psum_scatter(
        partial_value.astype(jnp.bfloat16), "index", scatter_dimension=1, tiled=True
    ).astype(jnp.float32)
    own_states = lax.dynamic_slice_in_dim(states, group_index * quarter, quarter, 1)
    layer = (own_states.astype(jnp.float32) + summed).astype(jnp.bfloat16)
    partial_pool = jnp.dot(member, layer, preferred_element_type=jnp.float32)
    pooled = lax.psum_scatter(
        partial_pool.astype(jnp.bfloat16), "seq", scatter_dimension=0, tiled=True
    ).astype(jnp.float32)
    shard_range = jnp.arange(index_count, dtype=jnp.int32)
    routing = (
        (shard_ids[None, None, :] == shard_range[:, None, None])
        & (slot_rank[None, None, :] == slot_ids[None, :, None])
    ).astype(jnp.float32)
    outgoing = jnp.einsum("rkc,cf->rkf", routing, pooled, precision=lax.Precision.HIGHEST)
    arrived = lax.all_to_all(outgoing, "index", split_axis=0, concat_axis=2, tiled=True)[0]
    shelf_rows = arrived * lax.rsqrt(jnp.mean(arrived * arrived, -1, keepdims=True) + 1e-06)
    return (layer[None], shelf_rows[None, None, None])


def lanes(shape):
    return lax.broadcasted_iota(jnp.int32, shape, 1)


def rotary(tile, cosine, sine):
    first = lanes(tile.shape) % HD < HD // 2
    partner = jnp.where(first, pltpu.roll(tile, 128 - HD // 2, 1), pltpu.roll(tile, HD // 2, 1))
    return tile * cosine + partner * sine


def folded(columns, odd):
    half = columns[0].shape[0] // 2
    low = lanes((half, 128)) < HD
    turn = lambda x: pltpu.roll(x, HD, 1)
    q, k, v = [[c[:half].astype(jnp.float32), c[half:].astype(jnp.float32)] for c in columns]
    parts = [jnp.where(low, jnp.where(odd, turn(q[p]), q[p]), jnp.where(odd, k[p], turn(k[p]))) for p in range(2)]
    parts.append(jnp.where(low, jnp.where(odd, turn(v[0]), v[0]), jnp.where(odd, v[1], turn(v[1]))))
    return jnp.concatenate(parts, 1).astype(columns[0].dtype)


def pieces_kernel(where, w_ref, x_ref, o_ref, out_ref, first_ref, second_ref, third_ref):
    out_ref[...] = o_ref[0]
    first_ref[...] = folded([w_ref[j] for j in range(3)], False)
    second_ref[...] = folded([w_ref[j] for j in range(3)], True)
    third_ref[...] = folded([x_ref[j] for j in range(3)], lax.rem(where[0], 2) == 1)


def pieces(where, proj_weight):
    _, shard, width = proj_weight.shape
    quarter = shard // 4
    return pl.pallas_call(
        pieces_kernel,
        grid_spec=pltpu.PrefetchScalarGridSpec(
            num_scalar_prefetch=1,
            grid=(1,),
            in_specs=[
                pl.BlockSpec((3, shard, 128), lambda i, where: (0, 0, where[0])),
                pl.BlockSpec((3, shard, 128), lambda i, where: (0, 0, 4 + where[0] // 2)),
                pl.BlockSpec((1, quarter, width), lambda i, where: (3, where[0], 0)),
            ],
            out_specs=[pl.BlockSpec((quarter, width), lambda i, where: (0, 0))]
            + [pl.BlockSpec((shard // 2, 384), lambda i, where: (0, 0))] * 3,
        ),
        out_shape=[jax.ShapeDtypeStruct((quarter, width), proj_weight.dtype)]
        + [jax.ShapeDtypeStruct((shard // 2, 384), proj_weight.dtype)] * 3,
        cost_estimate=SHORT,
        name="pieces",
    )(where, proj_weight, proj_weight, proj_weight)


def after(value, *earlier):
    return lax.optimization_barrier((value, *earlier))[0]


def members(lengths, positions):
    count = lengths.shape[1]
    shape = (count, count)
    row, other = lax.broadcasted_iota(jnp.int32, shape, 0), lax.broadcasted_iota(jnp.int32, shape, 1)
    per_block = count // 4
    stretch = lax.rem(row, per_block) * 4 + row // per_block
    values = jnp.broadcast_to(lengths, shape)
    ends = jnp.sum(jnp.where(other <= stretch, values, 0), 1, keepdims=True)
    starts = jnp.sum(jnp.where(other < stretch, values, 0), 1, keepdims=True)
    position = lax.broadcasted_iota(jnp.int32, (count, positions), 1)
    return jnp.where((position >= starts) & (position < ends), 1.0, 0.0).astype(jnp.bfloat16)


def attend_kernel(pools, *refs):
    where, h_refs, (cos_ref, sin_ref, lengths_ref), w_refs = refs[0], refs[1:5], refs[5:8], refs[8:12]
    out_refs = refs[12:16]
    q_s, k_s, v_s, c_s, member_s = refs[-5:]
    s, d, g = where[0], where[1], where[2]
    rows, d_model = h_refs[0].shape
    total = 4 * rows
    shard = d_model // 4
    half = shard // 2
    per_block = lengths_ref.shape[1] // 4
    member_s[...] = members(lengths_ref[...], total)

    for j in range(4):
        block = jnp.bitwise_xor(s, j)
        at = pl.ds(pl.multiple_of(block * rows, rows), rows)
        top = jnp.zeros((rows, 256), jnp.float32)
        bottom = jnp.zeros((rows, 256), jnp.float32)
        for k in range(4):
            column = lax.rem(d - k + 4, 4) * shard
            w = w_refs[k]
            h_top = h_refs[j][:, pl.ds(pl.multiple_of(column, half), half)]
            h_bottom = h_refs[j][:, pl.ds(pl.multiple_of(column + half, half), half)]
            top += jnp.dot(h_top, jnp.concatenate([w[:, 0:128], w[:, 256:384]], 1), preferred_element_type=jnp.float32)
            bottom += jnp.dot(h_bottom, w[:, 128:384], preferred_element_type=jnp.float32)
        qk = rotary(top[:, :128] + bottom[:, :128], cos_ref[at, :], sin_ref[at, :])
        low = lanes(qk.shape) < HD
        q_s[at, :] = jnp.where(low, qk * HD**-0.5, 0.0).astype(jnp.bfloat16)
        k_s[at, :] = pltpu.roll(qk, HD, 1).astype(jnp.bfloat16)
        v = top[:, 128:] + pltpu.roll(bottom[:, 128:], HD, 1)
        v_s[at, :] = jnp.where(low, v, 1.0).astype(jnp.bfloat16)

    step = 256
    for r in range(total // step):
        start, end = max(0, r * step - HALF_WIN), min(total, (r + 1) * step + HALF_WIN)
        ahead = lax.broadcasted_iota(jnp.int32, (step, step), 1) - lax.broadcasted_iota(jnp.int32, (step, step), 0)
        scores = lax.dot_general(
            q_s[r * step : (r + 1) * step, :], k_s[start:end, :], (((1,), (1,)), ((), ())), preferred_element_type=jnp.float32
        )
        parts = [scores]
        if start == r * step - HALF_WIN:
            parts = [jnp.where(ahead >= 0, scores[:, :step], -1e30), scores[:, step:]]
        if end == (r + 1) * step + HALF_WIN:
            last = parts.pop()
            parts += [last[:, :-step], jnp.where(ahead <= 0, last[:, -step:], -1e30)]
        scores = jnp.concatenate(parts, 1)
        expo = jnp.exp(scores - jnp.max(scores, 1, keepdims=True)).astype(jnp.bfloat16)
        o = jnp.dot(expo, v_s[start:end, :], preferred_element_type=jnp.float32)
        low = lanes(o.shape) < HD
        c_s[r * step : (r + 1) * step, :] = jnp.where(low, o / pltpu.roll(o, HD, 1), 0.0).astype(jnp.bfloat16)

    pooled = jnp.dot(member_s[...], c_s[...], preferred_element_type=jnp.float32)
    high = pooled.astype(jnp.bfloat16)
    rest = (pooled - high.astype(jnp.float32)).astype(jnp.bfloat16)
    for j in range(4):
        block = jnp.bitwise_xor(s, j)
        both = jnp.zeros((2 * per_block, 128), jnp.bfloat16)
        for b in range(4):
            cut = slice(b * per_block, (b + 1) * per_block)
            both = jnp.where(block == b, jnp.concatenate([high[cut], rest[cut]], 0), both)
        out = out_refs[j]
        lo = c_s[pl.ds(pl.multiple_of(block * rows, rows), rows // 2), :].astype(jnp.float32)
        hi = c_s[pl.ds(pl.multiple_of(block * rows + rows // 2, rows // 2), rows // 2), :].astype(jnp.float32)
        out[0 : rows // 2, :] = (lo + pltpu.roll(hi, HD, 1)).astype(jnp.bfloat16)
        out[rows // 2 :, :] = both

    if pools:
        feats = d_model // 2
        sums = jnp.zeros((4 * per_block, feats), jnp.float32)
        for j in range(4):
            rows_of = member_s[:, pl.ds(pl.multiple_of(jnp.bitwise_xor(s, j) * rows, rows), rows)]
            part = h_refs[j][:, pl.ds(pl.multiple_of(g * feats, feats), feats)]
            sums += jnp.dot(rows_of, part, preferred_element_type=jnp.float32)
        own = jnp.zeros((per_block, feats), jnp.float32)
        for b in range(4):
            own = jnp.where(s == b, sums[b * per_block : (b + 1) * per_block], own)
        refs[16][...] = own


def attend(where, blocks, tables, pieces, pools):
    rows, d_model = blocks[0].shape
    total = 4 * rows
    count = tables[2].shape[1]
    per_block = count // 4
    vmem = pl.BlockSpec(memory_space=pltpu.VMEM)
    out_shape = [jax.ShapeDtypeStruct((rows // 2 + 2 * per_block, 128), jnp.bfloat16)] * 4
    if pools:
        out_shape.append(jax.ShapeDtypeStruct((per_block, d_model // 2), jnp.float32))
    return pl.pallas_call(
        functools.partial(attend_kernel, pools),
        out_shape=out_shape,
        in_specs=[pl.BlockSpec(memory_space=pltpu.SMEM)] + [vmem] * 11,
        out_specs=[vmem] * len(out_shape),
        scratch_shapes=[pltpu.VMEM((total, 128), jnp.bfloat16)] * 4 + [pltpu.VMEM((count, total), jnp.bfloat16)],
        compiler_params=pltpu.CompilerParams(vmem_limit_bytes=24 * 2**20),
        cost_estimate=SHORT,
        name="attend_and_pool" if pools else "attend",
    )(where, *blocks, *tables, *pieces)


def merge(left, right, rows):
    left, right = left.astype(jnp.float32), right.astype(jnp.float32)
    low = lanes(left.shape) < HD
    first = jnp.where(low, left, pltpu.roll(right, HD, 1)).astype(jnp.bfloat16)
    second = jnp.where(low, pltpu.roll(left, HD, 1), right).astype(jnp.bfloat16)
    return first[: rows // 2], second[: rows // 2], first[rows // 2 :]


def project_tiles(s, d, c_s, four_ref, near_ref, columns):
    feats, width = four_ref.shape[2], columns[1] - columns[0]
    for p in range(2):
        in_half = lax.rem(lax.rem(d - p + 4, 4), 2)
        for j in range(4):
            source = near_ref if j % 2 else four_ref
            total = None
            for t in range(2):
                w = source[2 * (j // 2) + t, p, :, columns[0] : columns[1]]
                c = c_s[:, t * width : (t + 1) * width]
                product = lax.dot_general(c, w, (((1,), (1,)), ((), ())), preferred_element_type=jnp.float32)
                total = product if total is None else total + product
            yield pl.multiple_of((in_half * 4 + jnp.bitwise_xor(s, j)) * feats, 128), total


def early_kernel(where, *refs):
    firsts, seconds, (four_ref, near_ref, out_ref, c_s) = refs[0:5], refs[5:10], refs[10:]
    s, d = where[0], where[1]
    rows = 2 * (out_ref.shape[0] - firsts[0].shape[0])
    for t in range(2):
        for j in range(4):
            left, right = [r[j][...] if t == 0 else r[4][j] for r in (firsts, seconds)]
            top, bottom, sums = merge(left, right, rows)
            at = pl.ds(pl.multiple_of(t * 512 + jnp.bitwise_xor(s, j) * 128, 128), 128)
            c_s[0 : rows // 2, at] = top
            c_s[rows // 2 : rows, at] = bottom
            c_s[rows:, at] = sums
    for column, total in project_tiles(s, d, c_s, four_ref, near_ref, (0, 512)):
        out_ref[:, pl.ds(column, four_ref.shape[2])] = total


def project_early(where, first, second, weights):
    each = first[0].shape[0]
    feats = 8 * weights[0].shape[2]
    rows = weights[0].shape[2] * 2
    vmem = pl.BlockSpec(memory_space=pltpu.VMEM)
    return pl.pallas_call(
        early_kernel,
        out_shape=jax.ShapeDtypeStruct((each + rows // 2, feats), jnp.float32),
        in_specs=[pl.BlockSpec(memory_space=pltpu.SMEM)] + [vmem] * 12,
        out_specs=vmem,
        scratch_shapes=[pltpu.VMEM((each + rows // 2, 1024), jnp.bfloat16)],
        compiler_params=pltpu.CompilerParams(vmem_limit_bytes=24 * 2**20),
        cost_estimate=SHORT,
        name="project_early",
    )(where, *first, *second, *weights)


def late_kernel(where, shard_ref, h_ref, pool_ref, early_ref, *refs):
    thirds, (four_ref, near_ref, layer_ref, keep_ref, send_ref, c_s, o_s) = refs[0:5], refs[5:]
    s, d, g = where[0], where[1], where[2]
    rows = h_ref.shape[0]
    odd = jnp.bitwise_and(s, 1) == 1
    for t in range(2):
        parts = [thirds[j][...] if t == 0 else thirds[4][j] for j in range(4)]
        for pair in range(2):
            one, two = parts[2 * pair], parts[2 * pair + 1]
            top, bottom, sums = merge(jnp.where(odd, two, one), jnp.where(odd, one, two), rows)
            at = pl.ds(pl.multiple_of(t * 256 + jnp.bitwise_xor(s // 2, pair) * 128, 128), 128)
            c_s[0 : rows // 2, at] = top
            c_s[rows // 2 : rows, at] = bottom
            c_s[rows:, at] = sums

    feats = four_ref.shape[2]
    for column, total in project_tiles(s, d, c_s, four_ref, near_ref, (512, 768)):
        at = pl.ds(column, feats)
        total += early_ref[:, at]
        o_s[:, at] = total[rows:]
        mine = h_ref[:, pl.ds(pl.multiple_of(g * 8 * feats + column, 128), feats)]
        layer_ref[:, at] = (mine.astype(jnp.float32) + total[:rows]).astype(jnp.bfloat16)

    half = pool_ref.shape[0]
    pooled = pool_ref[...] + o_s[0:half] + o_s[half:]
    slots = 2 * keep_ref.shape[0]
    slot = lax.broadcasted_iota(jnp.int32, (slots, half), 0)
    source = lax.broadcasted_iota(jnp.int32, (slots, half), 1)
    route = jnp.zeros((slots, half), jnp.float32)
    ids = [shard_ref[c] for c in range(half)]
    for c in range(half):
        rank = sum([(ids[e] == ids[c]).astype(jnp.int32) for e in range(c)], jnp.int32(0))
        route = jnp.where((slot == ids[c] * (slots // 2) + rank) & (source == c), 1.0, route)
    routed = jnp.dot(route, pooled, precision=lax.Precision.HIGHEST, preferred_element_type=jnp.float32)
    cut = slots // 2
    keep_ref[...] = jnp.where(g == 0, routed[:cut], routed[cut:])
    send_ref[...] = jnp.where(g == 0, routed[cut:], routed[:cut])


def project_late(where, shard_ids, h, pool, early, third, weights):
    rows, d_model = h.shape
    feats = d_model // 2
    slots = shard_ids.shape[0] // 2
    vmem = pl.BlockSpec(memory_space=pltpu.VMEM)
    return pl.pallas_call(
        late_kernel,
        out_shape=[
            jax.ShapeDtypeStruct((rows, feats), jnp.bfloat16),
            jax.ShapeDtypeStruct((slots, feats), jnp.float32),
            jax.ShapeDtypeStruct((slots, feats), jnp.float32),
        ],
        in_specs=[pl.BlockSpec(memory_space=pltpu.SMEM)] * 2 + [vmem] * 10,
        out_specs=[vmem] * 3,
        scratch_shapes=[
            pltpu.VMEM((early.shape[0], 512), jnp.bfloat16),
            pltpu.VMEM((early.shape[0] - rows, feats), jnp.float32),
        ],
        compiler_params=pltpu.CompilerParams(vmem_limit_bytes=24 * 2**20),
        cost_estimate=SHORT,
        name="project_late",
    )(where, shard_ids, h, pool, early, *third, *weights)


def xor_send(name, value, axis, j):
    with jax.named_scope(name):
        return lax.ppermute(value, axis, [(i, i ^ j) for i in range(lax.axis_size(axis))])


def ring_send(name, value):
    count = lax.axis_size("dp")
    with jax.named_scope(name):
        return lax.ppermute(value, "dp", [(i, (i + 1) % count) for i in range(count)])


def rotary_tables(total):
    freqs = np.float32(10000.0) ** (np.float32(-2.0) * np.arange(HD // 2, dtype=np.float32) / np.float32(HD))
    angles = (np.arange(total, dtype=np.float32)[:, None] * freqs[None, :]).astype(np.float64)
    cosine, sine = np.cos(angles).astype(np.float32), np.sin(angles).astype(np.float32)
    return jnp.asarray(np.concatenate([cosine] * 4, 1)), jnp.asarray(np.concatenate([-sine, sine] * 2, 1))


def body_by_heads(hidden, proj_weight, stretch_lengths, shard_of):
    h = hidden[0]
    rows = h.shape[0]
    s, d, g = lax.axis_index("seq"), lax.axis_index("dp"), lax.axis_index("index")
    where = jnp.stack([s, d, g]).astype(jnp.int32)
    total = 4 * rows

    tables = (*rotary_tables(total), stretch_lengths)

    def across(ring):
        pairs = [((d - p) % 4 // 2 == g, ring[p], ring[p + 2]) for p in range(2)]
        keep = jnp.stack([jnp.where(mine, one, two) for mine, one, two in pairs])
        send = jnp.stack([jnp.where(mine, two, one) for mine, one, two in pairs])
        with jax.named_scope("out_across"):
            far = lax.ppermute(send, ("seq", "index"), [(i, i ^ 5) for i in range(8)])
        return keep, xor_send("out_group", send, "index", 1), xor_send("out_cross", keep, "seq", 2), far

    def to_seq(name, parts):
        return [parts[0]] + [xor_send(name, parts[j], "seq", j) for j in (1, 2, 3)]

    def to_other(name, parts):
        return parts + [xor_send(name, jnp.stack(parts), "index", 1)]

    h_cross = xor_send("hidden_cross", h, "seq", 2)
    h_core = xor_send("hidden_core", h, "seq", 1)
    o0, x0, y0, z0 = pieces(where, proj_weight)

    def rings(names, starts, **before):
        held = [[start] for start in starts]
        for step in range(3):
            for ring, name in zip(held, names):
                ring.append(ring_send(name, after(ring[-1], before[name]) if step == 1 and name in before else ring[-1]))
        return held

    out_ring, first_ring = rings(("out", "first"), (o0, x0))
    out_ring[3], first_ring[3], h_core, h_cross, y0, z0 = lax.optimization_barrier(
        (out_ring[3], first_ring[3], h_core, h_cross, y0, z0)
    )

    h_far = xor_send("hidden_far", h_cross, "seq", 1)
    second_ring, third_ring = rings(("second", "third"), (y0, z0), third=h_far)
    blocks = [h, h_core, h_cross, h_far]
    four = across(out_ring)
    first_ring[3] = after(first_ring[3], second_ring[2], third_ring[2])
    first = attend(where, blocks, tables, first_ring, True)
    first_parts = to_seq("context_first", first[:4])
    second = attend(where, blocks, tables, second_ring, False)
    third_ring[3], four, first_parts, second = lax.optimization_barrier((third_ring[3], four, first_parts, second))

    four = jnp.stack(four)
    near = xor_send("out_core", four, "seq", 1)
    first_parts = to_other("context_first_group", first_parts)
    second_parts = to_seq("context_second", second)
    third = attend(where, blocks, tables, third_ring, False)
    first_parts, second_parts, third, near = lax.optimization_barrier((first_parts, second_parts, third, near))

    second_parts = to_other("context_second_group", second_parts)
    third_parts = to_seq("context_third", third)
    second_parts[4] = after(second_parts[4], *third_parts)
    third_parts = to_other("context_third_group", third_parts)

    early = project_early(where, first_parts, second_parts, [four, near])
    layer, keep, send = project_late(where, shard_of[0, :, 0], h, first[4], early, third_parts, [four, near])
    arrived = xor_send("embedding_half", send, "index", 1)
    feats = keep.shape[1]
    square = (jnp.sum(keep * keep, -1, keepdims=True) + jnp.sum(arrived * arrived, -1, keepdims=True)) / (2 * feats)
    scale = lax.rsqrt(square + 1e-06)
    shelf = jnp.concatenate([jnp.where(g == 0, keep, arrived), jnp.where(g == 0, arrived, keep)], 1) * scale
    return (layer[None], shelf[None, None, None])


def solution(mesh):
    in_specs = (P("dp", "seq", None), P(None, "dp", "index"), P("dp", None), P("dp", "seq", None))
    out_specs = (P("dp", "seq", "index"), P("dp", "seq", "index", None, None))

    def whole(hidden, proj_weight, stretch_lengths, shard_of):
        heads = proj_weight.shape[2] // HD // mesh.shape["index"]
        rows = hidden.shape[1] // mesh.shape["seq"]
        by_heads = (mesh.shape["dp"], mesh.shape["seq"], mesh.shape["index"], heads, rows) == (4, 4, 2, 12, 256)
        return jax.shard_map(
            body_by_heads if by_heads else body,
            mesh=mesh,
            in_specs=in_specs,
            out_specs=out_specs,
            check_vma=False,
        )(hidden, proj_weight, stretch_lengths, shard_of)

    return whole
```

```python
import functools

import jax
import jax.numpy as jnp
import numpy as np
from jax import lax
from jax.experimental import pallas as pl
from jax.experimental.pallas import tpu as pltpu
from jax.sharding import PartitionSpec as P

D = 2048
HD = 64
HALF_WIN = 256

SHORT = pl.CostEstimate(flops=1, bytes_accessed=1, transcendentals=0)


def with_halo(cells, sides, width):
    for axis, dim in sides:
        count = lax.axis_size(axis)
        ends = count - 1
        head = lax.slice_in_dim(cells, 0, width, axis=dim)
        tail = lax.slice_in_dim(cells, cells.shape[dim] - width, cells.shape[dim], axis=dim)
        cells = jnp.concatenate(
            [
                lax.ppermute(tail, axis, [(i, (i + 1) % count) for i in range(ends)]),
                cells,
                lax.ppermute(head, axis, [((i + 1) % count, i) for i in range(ends)]),
            ],
            axis=dim,
        )
    return cells


def rotate(values_in, positions):
    half_dim = HD // 2
    freqs = 10000.0 ** (-2.0 * jnp.arange(half_dim, dtype=jnp.float32) / HD)
    angles = positions.astype(jnp.float32)[:, None] * freqs[None, :]
    cosine = jnp.cos(angles)[:, None, :]
    sine = jnp.sin(angles)[:, None, :]
    first = values_in[..., :half_dim]
    second = values_in[..., half_dim:]
    return jnp.concatenate([first * cosine - second * sine, second * cosine + first * sine], -1)


def window_heads(queries, key_rows, value_rows, visible):
    scale = HD ** (-0.5)

    def one_head(items):
        query_head, key_head, value_head = items
        scores = jnp.dot(query_head, key_head.T, preferred_element_type=jnp.float32) * scale
        scores = jnp.where(visible, scores, -1e30)
        maxima = jnp.max(scores, -1, keepdims=True)
        expo = jnp.exp(scores - maxima)
        weights = (expo / jnp.sum(expo, -1, keepdims=True)).astype(jnp.bfloat16)
        return jnp.dot(weights, value_head, preferred_element_type=jnp.float32).astype(jnp.bfloat16)

    context = lax.map(
        one_head,
        (jnp.moveaxis(queries, 1, 0), jnp.moveaxis(key_rows, 1, 0), jnp.moveaxis(value_rows, 1, 0)),
    )
    return jnp.moveaxis(context, 0, 1)


def body(hidden, proj_weight, stretch_lengths, shard_of):
    states = hidden[0]
    tokens_here = states.shape[0]
    width = proj_weight.shape[2]
    heads_here = width // HD
    seq_index = lax.axis_index("seq")
    group_index = lax.axis_index("index")
    seq_count = lax.axis_size("seq")
    index_count = lax.axis_size("index")
    total_length = tokens_here * seq_count
    positions = seq_index * tokens_here + jnp.arange(tokens_here, dtype=jnp.int32)
    projected = jnp.einsum(
        "td,jdc->jtc",
        states,
        lax.all_gather(proj_weight[:3], "dp", axis=1, tiled=True),
        preferred_element_type=jnp.float32,
    )
    queries = rotate(projected[0].reshape(tokens_here, heads_here, HD), positions).astype(
        jnp.bfloat16
    )
    key_rows = rotate(projected[1].reshape(tokens_here, heads_here, HD), positions).astype(
        jnp.bfloat16
    )
    value_rows = projected[2].astype(jnp.bfloat16)
    stacked = jnp.stack([key_rows.reshape(tokens_here, width), value_rows])
    padded = with_halo(stacked, (("seq", 1),), HALF_WIN)
    span = tokens_here + 2 * HALF_WIN
    key_part = padded[0, 0:span].reshape(span, heads_here, HD)
    value_part = padded[1, 0:span].reshape(span, heads_here, HD)
    key_pos = seq_index * tokens_here + 0 - HALF_WIN + jnp.arange(span, dtype=jnp.int32)
    visible = (
        (jnp.abs(key_pos[None, :] - positions[:, None]) <= HALF_WIN)
        & (key_pos[None, :] >= 0)
        & (key_pos[None, :] < total_length)
    )
    context_parts = window_heads(queries, key_part, value_part, visible).reshape(tokens_here, width)
    partial_value = lax.dot_general(
        context_parts,
        lax.all_gather(proj_weight[3], "dp", axis=0, tiled=True),
        (((1,), (1,)), ((), ())),
        preferred_element_type=jnp.float32,
    )
    lengths = stretch_lengths[0]
    stretch_count = lengths.shape[0]
    per_block = stretch_count // seq_count
    ends = jnp.cumsum(lengths, dtype=jnp.int32)
    starts = ends - lengths
    row_ids = jnp.arange(stretch_count, dtype=jnp.int32)
    order = row_ids % per_block * seq_count + row_ids // per_block
    row_starts = starts[order]
    row_ends = ends[order]
    member = (
        (positions[None, :] >= row_starts[:, None]) & (positions[None, :] < row_ends[:, None])
    ).astype(jnp.bfloat16)
    shard_ids = shard_of[0, :, 0]
    local_rows = jnp.arange(per_block, dtype=jnp.int32)
    earlier = (shard_ids[:, None] == shard_ids[None, :]) & (
        local_rows[None, :] < local_rows[:, None]
    )
    slot_rank = jnp.sum(earlier.astype(jnp.int32), 1)
    capacity = per_block // 2
    slot_ids = jnp.arange(capacity, dtype=jnp.int32)
    quarter = D // index_count
    summed = lax.psum_scatter(
        partial_value.astype(jnp.bfloat16), "index", scatter_dimension=1, tiled=True
    ).astype(jnp.float32)
    own_states = lax.dynamic_slice_in_dim(states, group_index * quarter, quarter, 1)
    layer = (own_states.astype(jnp.float32) + summed).astype(jnp.bfloat16)
    partial_pool = jnp.dot(member, layer, preferred_element_type=jnp.float32)
    pooled = lax.psum_scatter(
        partial_pool.astype(jnp.bfloat16), "seq", scatter_dimension=0, tiled=True
    ).astype(jnp.float32)
    shard_range = jnp.arange(index_count, dtype=jnp.int32)
    routing = (
        (shard_ids[None, None, :] == shard_range[:, None, None])
        & (slot_rank[None, None, :] == slot_ids[None, :, None])
    ).astype(jnp.float32)
    outgoing = jnp.einsum("rkc,cf->rkf", routing, pooled, precision=lax.Precision.HIGHEST)
    arrived = lax.all_to_all(outgoing, "index", split_axis=0, concat_axis=2, tiled=True)[0]
    shelf_rows = arrived * lax.rsqrt(jnp.mean(arrived * arrived, -1, keepdims=True) + 1e-06)
    return (layer[None], shelf_rows[None, None, None])


def lanes(shape):
    return lax.broadcasted_iota(jnp.int32, shape, 1)


def rotary(tile, cosine, sine):
    first = lanes(tile.shape) % HD < HD // 2
    partner = jnp.where(first, pltpu.roll(tile, 128 - HD // 2, 1), pltpu.roll(tile, HD // 2, 1))
    return tile * cosine + partner * sine


def folded(columns, odd):
    half = columns[0].shape[0] // 2
    low = lanes((half, 128)) < HD
    turn = lambda x: pltpu.roll(x, HD, 1)
    q, k, v = [[c[:half].astype(jnp.float32), c[half:].astype(jnp.float32)] for c in columns]
    parts = [jnp.where(low, jnp.where(odd, turn(q[p]), q[p]), jnp.where(odd, k[p], turn(k[p]))) for p in range(2)]
    parts.append(jnp.where(low, jnp.where(odd, turn(v[0]), v[0]), jnp.where(odd, v[1], turn(v[1]))))
    return jnp.concatenate(parts, 1).astype(columns[0].dtype)


def pieces_kernel(where, w_ref, x_ref, o_ref, out_ref, first_ref, second_ref, third_ref):
    out_ref[...] = o_ref[0]
    first_ref[...] = folded([w_ref[j] for j in range(3)], False)
    second_ref[...] = folded([w_ref[j] for j in range(3)], True)
    third_ref[...] = folded([x_ref[j] for j in range(3)], lax.rem(where[0], 2) == 1)


def pieces(where, proj_weight):
    _, shard, width = proj_weight.shape
    quarter = shard // 4
    return pl.pallas_call(
        pieces_kernel,
        grid_spec=pltpu.PrefetchScalarGridSpec(
            num_scalar_prefetch=1,
            grid=(1,),
            in_specs=[
                pl.BlockSpec((3, shard, 128), lambda i, where: (0, 0, where[0])),
                pl.BlockSpec((3, shard, 128), lambda i, where: (0, 0, 4 + where[0] // 2)),
                pl.BlockSpec((1, quarter, width), lambda i, where: (3, where[0], 0)),
            ],
            out_specs=[pl.BlockSpec((quarter, width), lambda i, where: (0, 0))]
            + [pl.BlockSpec((shard // 2, 384), lambda i, where: (0, 0))] * 3,
        ),
        out_shape=[jax.ShapeDtypeStruct((quarter, width), proj_weight.dtype)]
        + [jax.ShapeDtypeStruct((shard // 2, 384), proj_weight.dtype)] * 3,
        cost_estimate=SHORT,
        name="pieces",
    )(where, proj_weight, proj_weight, proj_weight)


def after(value, *earlier):
    return lax.optimization_barrier((value, *earlier))[0]


def members(lengths, positions):
    count = lengths.shape[1]
    shape = (count, count)
    row, other = lax.broadcasted_iota(jnp.int32, shape, 0), lax.broadcasted_iota(jnp.int32, shape, 1)
    per_block = count // 4
    stretch = lax.rem(row, per_block) * 4 + row // per_block
    values = jnp.broadcast_to(lengths, shape)
    ends = jnp.sum(jnp.where(other <= stretch, values, 0), 1, keepdims=True)
    starts = jnp.sum(jnp.where(other < stretch, values, 0), 1, keepdims=True)
    position = lax.broadcasted_iota(jnp.int32, (count, positions), 1)
    return jnp.where((position >= starts) & (position < ends), 1.0, 0.0).astype(jnp.bfloat16)


def attend_kernel(pools, *refs):
    where, h_refs, (cos_ref, sin_ref, lengths_ref), w_refs = refs[0], refs[1:5], refs[5:8], refs[8:12]
    out_refs = refs[12:16]
    q_s, k_s, v_s, c_s, member_s = refs[-5:]
    s, d, g = where[0], where[1], where[2]
    rows, d_model = h_refs[0].shape
    total = 4 * rows
    shard = d_model // 4
    half = shard // 2
    per_block = lengths_ref.shape[1] // 4
    member_s[...] = members(lengths_ref[...], total)

    for j in range(4):
        block = jnp.bitwise_xor(s, j)
        at = pl.ds(pl.multiple_of(block * rows, rows), rows)
        top = jnp.zeros((rows, 256), jnp.float32)
        bottom = jnp.zeros((rows, 256), jnp.float32)
        for k in range(4):
            column = lax.rem(d - k + 4, 4) * shard
            w = w_refs[k]
            h_top = h_refs[j][:, pl.ds(pl.multiple_of(column, half), half)]
            h_bottom = h_refs[j][:, pl.ds(pl.multiple_of(column + half, half), half)]
            top += jnp.dot(h_top, jnp.concatenate([w[:, 0:128], w[:, 256:384]], 1), preferred_element_type=jnp.float32)
            bottom += jnp.dot(h_bottom, w[:, 128:384], preferred_element_type=jnp.float32)
        qk = rotary(top[:, :128] + bottom[:, :128], cos_ref[at, :], sin_ref[at, :])
        low = lanes(qk.shape) < HD
        q_s[at, :] = jnp.where(low, qk * HD**-0.5, 0.0).astype(jnp.bfloat16)
        k_s[at, :] = pltpu.roll(qk, HD, 1).astype(jnp.bfloat16)
        v = top[:, 128:] + pltpu.roll(bottom[:, 128:], HD, 1)
        v_s[at, :] = jnp.where(low, v, 1.0).astype(jnp.bfloat16)

    step = 256
    for r in range(total // step):
        start, end = max(0, r * step - HALF_WIN), min(total, (r + 1) * step + HALF_WIN)
        ahead = lax.broadcasted_iota(jnp.int32, (step, step), 1) - lax.broadcasted_iota(jnp.int32, (step, step), 0)
        scores = lax.dot_general(
            q_s[r * step : (r + 1) * step, :], k_s[start:end, :], (((1,), (1,)), ((), ())), preferred_element_type=jnp.float32
        )
        parts = [scores]
        if start == r * step - HALF_WIN:
            parts = [jnp.where(ahead >= 0, scores[:, :step], -1e30), scores[:, step:]]
        if end == (r + 1) * step + HALF_WIN:
            last = parts.pop()
            parts += [last[:, :-step], jnp.where(ahead <= 0, last[:, -step:], -1e30)]
        scores = jnp.concatenate(parts, 1)
        expo = jnp.exp(scores - jnp.max(scores, 1, keepdims=True)).astype(jnp.bfloat16)
        o = jnp.dot(expo, v_s[start:end, :], preferred_element_type=jnp.float32)
        low = lanes(o.shape) < HD
        c_s[r * step : (r + 1) * step, :] = jnp.where(low, o / pltpu.roll(o, HD, 1), 0.0).astype(jnp.bfloat16)

    pooled = jnp.dot(member_s[...], c_s[...], preferred_element_type=jnp.float32)
    high = pooled.astype(jnp.bfloat16)
    rest = (pooled - high.astype(jnp.float32)).astype(jnp.bfloat16)
    for j in range(4):
        block = jnp.bitwise_xor(s, j)
        both = jnp.zeros((2 * per_block, 128), jnp.bfloat16)
        for b in range(4):
            cut = slice(b * per_block, (b + 1) * per_block)
            both = jnp.where(block == b, jnp.concatenate([high[cut], rest[cut]], 0), both)
        out = out_refs[j]
        lo = c_s[pl.ds(pl.multiple_of(block * rows, rows), rows // 2), :].astype(jnp.float32)
        hi = c_s[pl.ds(pl.multiple_of(block * rows + rows // 2, rows // 2), rows // 2), :].astype(jnp.float32)
        out[0 : rows // 2, :] = (lo + pltpu.roll(hi, HD, 1)).astype(jnp.bfloat16)
        out[rows // 2 :, :] = both

    if pools:
        feats = d_model // 2
        sums = jnp.zeros((4 * per_block, feats), jnp.float32)
        for j in range(4):
            rows_of = member_s[:, pl.ds(pl.multiple_of(jnp.bitwise_xor(s, j) * rows, rows), rows)]
            part = h_refs[j][:, pl.ds(pl.multiple_of(g * feats, feats), feats)]
            sums += jnp.dot(rows_of, part, preferred_element_type=jnp.float32)
        own = jnp.zeros((per_block, feats), jnp.float32)
        for b in range(4):
            own = jnp.where(s == b, sums[b * per_block : (b + 1) * per_block], own)
        refs[16][...] = own


def attend(where, blocks, tables, pieces, pools):
    rows, d_model = blocks[0].shape
    total = 4 * rows
    count = tables[2].shape[1]
    per_block = count // 4
    vmem = pl.BlockSpec(memory_space=pltpu.VMEM)
    out_shape = [jax.ShapeDtypeStruct((rows // 2 + 2 * per_block, 128), jnp.bfloat16)] * 4
    if pools:
        out_shape.append(jax.ShapeDtypeStruct((per_block, d_model // 2), jnp.float32))
    return pl.pallas_call(
        functools.partial(attend_kernel, pools),
        out_shape=out_shape,
        in_specs=[pl.BlockSpec(memory_space=pltpu.SMEM)] + [vmem] * 11,
        out_specs=[vmem] * len(out_shape),
        scratch_shapes=[pltpu.VMEM((total, 128), jnp.bfloat16)] * 4 + [pltpu.VMEM((count, total), jnp.bfloat16)],
        compiler_params=pltpu.CompilerParams(vmem_limit_bytes=24 * 2**20),
        cost_estimate=SHORT,
        name="attend_and_pool" if pools else "attend",
    )(where, *blocks, *tables, *pieces)


def merge(left, right, rows):
    left, right = left.astype(jnp.float32), right.astype(jnp.float32)
    low = lanes(left.shape) < HD
    first = jnp.where(low, left, pltpu.roll(right, HD, 1)).astype(jnp.bfloat16)
    second = jnp.where(low, pltpu.roll(left, HD, 1), right).astype(jnp.bfloat16)
    return first[: rows // 2], second[: rows // 2], first[rows // 2 :]


def project_tiles(s, d, c_s, four_ref, near_ref, columns):
    feats, width = four_ref.shape[2], columns[1] - columns[0]
    for p in range(2):
        in_half = lax.rem(lax.rem(d - p + 4, 4), 2)
        for j in range(4):
            source = near_ref if j % 2 else four_ref
            total = None
            for t in range(2):
                w = source[2 * (j // 2) + t, p, :, columns[0] : columns[1]]
                c = c_s[:, t * width : (t + 1) * width]
                product = lax.dot_general(c, w, (((1,), (1,)), ((), ())), preferred_element_type=jnp.float32)
                total = product if total is None else total + product
            yield pl.multiple_of((in_half * 4 + jnp.bitwise_xor(s, j)) * feats, 128), total


def early_kernel(where, *refs):
    firsts, seconds, (four_ref, near_ref, out_ref, c_s) = refs[0:5], refs[5:10], refs[10:]
    s, d = where[0], where[1]
    rows = 2 * (out_ref.shape[0] - firsts[0].shape[0])
    for t in range(2):
        for j in range(4):
            left, right = [r[j][...] if t == 0 else r[4][j] for r in (firsts, seconds)]
            top, bottom, sums = merge(left, right, rows)
            at = pl.ds(pl.multiple_of(t * 512 + jnp.bitwise_xor(s, j) * 128, 128), 128)
            c_s[0 : rows // 2, at] = top
            c_s[rows // 2 : rows, at] = bottom
            c_s[rows:, at] = sums
    for column, total in project_tiles(s, d, c_s, four_ref, near_ref, (0, 512)):
        out_ref[:, pl.ds(column, four_ref.shape[2])] = total


def project_early(where, first, second, weights):
    each = first[0].shape[0]
    feats = 8 * weights[0].shape[2]
    rows = weights[0].shape[2] * 2
    vmem = pl.BlockSpec(memory_space=pltpu.VMEM)
    return pl.pallas_call(
        early_kernel,
        out_shape=jax.ShapeDtypeStruct((each + rows // 2, feats), jnp.float32),
        in_specs=[pl.BlockSpec(memory_space=pltpu.SMEM)] + [vmem] * 12,
        out_specs=vmem,
        scratch_shapes=[pltpu.VMEM((each + rows // 2, 1024), jnp.bfloat16)],
        compiler_params=pltpu.CompilerParams(vmem_limit_bytes=24 * 2**20),
        cost_estimate=SHORT,
        name="project_early",
    )(where, *first, *second, *weights)


def late_kernel(where, shard_ref, h_ref, pool_ref, early_ref, *refs):
    thirds, (four_ref, near_ref, layer_ref, keep_ref, send_ref, c_s, o_s) = refs[0:5], refs[5:]
    s, d, g = where[0], where[1], where[2]
    rows = h_ref.shape[0]
    odd = jnp.bitwise_and(s, 1) == 1
    for t in range(2):
        parts = [thirds[j][...] if t == 0 else thirds[4][j] for j in range(4)]
        for pair in range(2):
            one, two = parts[2 * pair], parts[2 * pair + 1]
            top, bottom, sums = merge(jnp.where(odd, two, one), jnp.where(odd, one, two), rows)
            at = pl.ds(pl.multiple_of(t * 256 + jnp.bitwise_xor(s // 2, pair) * 128, 128), 128)
            c_s[0 : rows // 2, at] = top
            c_s[rows // 2 : rows, at] = bottom
            c_s[rows:, at] = sums

    feats = four_ref.shape[2]
    for column, total in project_tiles(s, d, c_s, four_ref, near_ref, (512, 768)):
        at = pl.ds(column, feats)
        total += early_ref[:, at]
        o_s[:, at] = total[rows:]
        mine = h_ref[:, pl.ds(pl.multiple_of(g * 8 * feats + column, 128), feats)]
        layer_ref[:, at] = (mine.astype(jnp.float32) + total[:rows]).astype(jnp.bfloat16)

    half = pool_ref.shape[0]
    pooled = pool_ref[...] + o_s[0:half] + o_s[half:]
    slots = 2 * keep_ref.shape[0]
    slot = lax.broadcasted_iota(jnp.int32, (slots, half), 0)
    source = lax.broadcasted_iota(jnp.int32, (slots, half), 1)
    route = jnp.zeros((slots, half), jnp.float32)
    ids = [shard_ref[c] for c in range(half)]
    for c in range(half):
        rank = sum([(ids[e] == ids[c]).astype(jnp.int32) for e in range(c)], jnp.int32(0))
        route = jnp.where((slot == ids[c] * (slots // 2) + rank) & (source == c), 1.0, route)
    routed = jnp.dot(route, pooled, precision=lax.Precision.HIGHEST, preferred_element_type=jnp.float32)
    cut = slots // 2
    keep_ref[...] = jnp.where(g == 0, routed[:cut], routed[cut:])
    send_ref[...] = jnp.where(g == 0, routed[cut:], routed[:cut])


def project_late(where, shard_ids, h, pool, early, third, weights):
    rows, d_model = h.shape
    feats = d_model // 2
    slots = shard_ids.shape[0] // 2
    vmem = pl.BlockSpec(memory_space=pltpu.VMEM)
    return pl.pallas_call(
        late_kernel,
        out_shape=[
            jax.ShapeDtypeStruct((rows, feats), jnp.bfloat16),
            jax.ShapeDtypeStruct((slots, feats), jnp.float32),
            jax.ShapeDtypeStruct((slots, feats), jnp.float32),
        ],
        in_specs=[pl.BlockSpec(memory_space=pltpu.SMEM)] * 2 + [vmem] * 10,
        out_specs=[vmem] * 3,
        scratch_shapes=[
            pltpu.VMEM((early.shape[0], 512), jnp.bfloat16),
            pltpu.VMEM((early.shape[0] - rows, feats), jnp.float32),
        ],
        compiler_params=pltpu.CompilerParams(vmem_limit_bytes=24 * 2**20),
        cost_estimate=SHORT,
        name="project_late",
    )(where, shard_ids, h, pool, early, *third, *weights)


def xor_send(name, value, axis, j):
    with jax.named_scope(name):
        return lax.ppermute(value, axis, [(i, i ^ j) for i in range(lax.axis_size(axis))])


def ring_send(name, value):
    count = lax.axis_size("dp")
    with jax.named_scope(name):
        return lax.ppermute(value, "dp", [(i, (i + 1) % count) for i in range(count)])


def rotary_tables(total):
    freqs = np.float32(10000.0) ** (np.float32(-2.0) * np.arange(HD // 2, dtype=np.float32) / np.float32(HD))
    angles = (np.arange(total, dtype=np.float32)[:, None] * freqs[None, :]).astype(np.float64)
    cosine, sine = np.cos(angles).astype(np.float32), np.sin(angles).astype(np.float32)
    return jnp.asarray(np.concatenate([cosine] * 4, 1)), jnp.asarray(np.concatenate([-sine, sine] * 2, 1))


def body_by_heads(hidden, proj_weight, stretch_lengths, shard_of):
    h = hidden[0]
    rows = h.shape[0]
    s, d, g = lax.axis_index("seq"), lax.axis_index("dp"), lax.axis_index("index")
    where = jnp.stack([s, d, g]).astype(jnp.int32)
    total = 4 * rows

    tables = (*rotary_tables(total), stretch_lengths)

    def across(ring):
        pairs = [((d - p) % 4 // 2 == g, ring[p], ring[p + 2]) for p in range(2)]
        keep = jnp.stack([jnp.where(mine, one, two) for mine, one, two in pairs])
        send = jnp.stack([jnp.where(mine, two, one) for mine, one, two in pairs])
        with jax.named_scope("out_across"):
            far = lax.ppermute(send, ("seq", "index"), [(i, i ^ 5) for i in range(8)])
        return keep, xor_send("out_group", send, "index", 1), xor_send("out_cross", keep, "seq", 2), far

    def to_seq(name, parts):
        return [parts[0]] + [xor_send(name, parts[j], "seq", j) for j in (1, 2, 3)]

    def to_other(name, parts):
        return parts + [xor_send(name, jnp.stack(parts), "index", 1)]

    h_cross = xor_send("hidden_cross", h, "seq", 2)
    h_core = xor_send("hidden_core", h, "seq", 1)
    o0, x0, y0, z0 = pieces(where, proj_weight)

    def rings(names, starts, **before):
        held = [[start] for start in starts]
        for step in range(3):
            for ring, name in zip(held, names):
                ring.append(ring_send(name, after(ring[-1], before[name]) if step == 1 and name in before else ring[-1]))
        return held

    out_ring, first_ring = rings(("out", "first"), (o0, x0))
    out_ring[3], first_ring[3], h_core, h_cross, y0, z0 = lax.optimization_barrier(
        (out_ring[3], first_ring[3], h_core, h_cross, y0, z0)
    )

    h_far = xor_send("hidden_far", h_cross, "seq", 1)
    y1, z1 = ring_send("second", y0), ring_send("third", z0)
    y2, z2 = ring_send("second", y1), ring_send("third", after(z1, h_far))
    blocks = [h, h_core, h_cross, h_far]
    four = across(out_ring)
    first_ring[3] = after(first_ring[3], y1, z1)
    first = attend(where, blocks, tables, first_ring, True)
    y3, z3 = ring_send("second", after(y2)), ring_send("third", after(z2, first[4]))
    second_ring, third_ring = [y0, y1, y2, y3], [z0, z1, z2, z3]
    first_parts = to_seq("context_first", first[:4])
    second = attend(where, blocks, tables, second_ring, False)
    third_ring[3], four, first_parts, second = lax.optimization_barrier((third_ring[3], four, first_parts, second))

    four = jnp.stack(four)
    near = xor_send("out_core", four, "seq", 1)
    first_parts = to_other("context_first_group", first_parts)
    second_parts = to_seq("context_second", second)
    third = attend(where, blocks, tables, third_ring, False)
    first_parts, second_parts, third, near = lax.optimization_barrier((first_parts, second_parts, third, near))

    second_parts = to_other("context_second_group", second_parts)
    third_parts = to_seq("context_third", third)
    second_parts[4] = after(second_parts[4], *third_parts)
    third_parts = to_other("context_third_group", third_parts)

    early = project_early(where, first_parts, second_parts, [four, near])
    layer, keep, send = project_late(where, shard_of[0, :, 0], h, first[4], early, third_parts, [four, near])
    arrived = xor_send("embedding_half", send, "index", 1)
    feats = keep.shape[1]
    square = (jnp.sum(keep * keep, -1, keepdims=True) + jnp.sum(arrived * arrived, -1, keepdims=True)) / (2 * feats)
    scale = lax.rsqrt(square + 1e-06)
    shelf = jnp.concatenate([jnp.where(g == 0, keep, arrived), jnp.where(g == 0, arrived, keep)], 1) * scale
    return (layer[None], shelf[None, None, None])


def solution(mesh):
    in_specs = (P("dp", "seq", None), P(None, "dp", "index"), P("dp", None), P("dp", "seq", None))
    out_specs = (P("dp", "seq", "index"), P("dp", "seq", "index", None, None))

    def whole(hidden, proj_weight, stretch_lengths, shard_of):
        heads = proj_weight.shape[2] // HD // mesh.shape["index"]
        rows = hidden.shape[1] // mesh.shape["seq"]
        by_heads = (mesh.shape["dp"], mesh.shape["seq"], mesh.shape["index"], heads, rows) == (4, 4, 2, 12, 256)
        return jax.shard_map(
            body_by_heads if by_heads else body,
            mesh=mesh,
            in_specs=in_specs,
            out_specs=out_specs,
            check_vma=False,
        )(hidden, proj_weight, stretch_lengths, shard_of)

    return whole
```

```python
import functools

import jax
import jax.numpy as jnp
import numpy as np
from jax import lax
from jax.experimental import pallas as pl
from jax.experimental.pallas import tpu as pltpu
from jax.sharding import PartitionSpec as P

D = 2048
HD = 64
HALF_WIN = 256

SHORT = pl.CostEstimate(flops=1, bytes_accessed=1, transcendentals=0)


def with_halo(cells, sides, width):
    for axis, dim in sides:
        count = lax.axis_size(axis)
        ends = count - 1
        head = lax.slice_in_dim(cells, 0, width, axis=dim)
        tail = lax.slice_in_dim(cells, cells.shape[dim] - width, cells.shape[dim], axis=dim)
        cells = jnp.concatenate(
            [
                lax.ppermute(tail, axis, [(i, (i + 1) % count) for i in range(ends)]),
                cells,
                lax.ppermute(head, axis, [((i + 1) % count, i) for i in range(ends)]),
            ],
            axis=dim,
        )
    return cells


def rotate(values_in, positions):
    half_dim = HD // 2
    freqs = 10000.0 ** (-2.0 * jnp.arange(half_dim, dtype=jnp.float32) / HD)
    angles = positions.astype(jnp.float32)[:, None] * freqs[None, :]
    cosine = jnp.cos(angles)[:, None, :]
    sine = jnp.sin(angles)[:, None, :]
    first = values_in[..., :half_dim]
    second = values_in[..., half_dim:]
    return jnp.concatenate([first * cosine - second * sine, second * cosine + first * sine], -1)


def window_heads(queries, key_rows, value_rows, visible):
    scale = HD ** (-0.5)

    def one_head(items):
        query_head, key_head, value_head = items
        scores = jnp.dot(query_head, key_head.T, preferred_element_type=jnp.float32) * scale
        scores = jnp.where(visible, scores, -1e30)
        maxima = jnp.max(scores, -1, keepdims=True)
        expo = jnp.exp(scores - maxima)
        weights = (expo / jnp.sum(expo, -1, keepdims=True)).astype(jnp.bfloat16)
        return jnp.dot(weights, value_head, preferred_element_type=jnp.float32).astype(jnp.bfloat16)

    context = lax.map(
        one_head,
        (jnp.moveaxis(queries, 1, 0), jnp.moveaxis(key_rows, 1, 0), jnp.moveaxis(value_rows, 1, 0)),
    )
    return jnp.moveaxis(context, 0, 1)


def body(hidden, proj_weight, stretch_lengths, shard_of):
    states = hidden[0]
    tokens_here = states.shape[0]
    width = proj_weight.shape[2]
    heads_here = width // HD
    seq_index = lax.axis_index("seq")
    group_index = lax.axis_index("index")
    seq_count = lax.axis_size("seq")
    index_count = lax.axis_size("index")
    total_length = tokens_here * seq_count
    positions = seq_index * tokens_here + jnp.arange(tokens_here, dtype=jnp.int32)
    projected = jnp.einsum(
        "td,jdc->jtc",
        states,
        lax.all_gather(proj_weight[:3], "dp", axis=1, tiled=True),
        preferred_element_type=jnp.float32,
    )
    queries = rotate(projected[0].reshape(tokens_here, heads_here, HD), positions).astype(
        jnp.bfloat16
    )
    key_rows = rotate(projected[1].reshape(tokens_here, heads_here, HD), positions).astype(
        jnp.bfloat16
    )
    value_rows = projected[2].astype(jnp.bfloat16)
    stacked = jnp.stack([key_rows.reshape(tokens_here, width), value_rows])
    padded = with_halo(stacked, (("seq", 1),), HALF_WIN)
    span = tokens_here + 2 * HALF_WIN
    key_part = padded[0, 0:span].reshape(span, heads_here, HD)
    value_part = padded[1, 0:span].reshape(span, heads_here, HD)
    key_pos = seq_index * tokens_here + 0 - HALF_WIN + jnp.arange(span, dtype=jnp.int32)
    visible = (
        (jnp.abs(key_pos[None, :] - positions[:, None]) <= HALF_WIN)
        & (key_pos[None, :] >= 0)
        & (key_pos[None, :] < total_length)
    )
    context_parts = window_heads(queries, key_part, value_part, visible).reshape(tokens_here, width)
    partial_value = lax.dot_general(
        context_parts,
        lax.all_gather(proj_weight[3], "dp", axis=0, tiled=True),
        (((1,), (1,)), ((), ())),
        preferred_element_type=jnp.float32,
    )
    lengths = stretch_lengths[0]
    stretch_count = lengths.shape[0]
    per_block = stretch_count // seq_count
    ends = jnp.cumsum(lengths, dtype=jnp.int32)
    starts = ends - lengths
    row_ids = jnp.arange(stretch_count, dtype=jnp.int32)
    order = row_ids % per_block * seq_count + row_ids // per_block
    row_starts = starts[order]
    row_ends = ends[order]
    member = (
        (positions[None, :] >= row_starts[:, None]) & (positions[None, :] < row_ends[:, None])
    ).astype(jnp.bfloat16)
    shard_ids = shard_of[0, :, 0]
    local_rows = jnp.arange(per_block, dtype=jnp.int32)
    earlier = (shard_ids[:, None] == shard_ids[None, :]) & (
        local_rows[None, :] < local_rows[:, None]
    )
    slot_rank = jnp.sum(earlier.astype(jnp.int32), 1)
    capacity = per_block // 2
    slot_ids = jnp.arange(capacity, dtype=jnp.int32)
    quarter = D // index_count
    summed = lax.psum_scatter(
        partial_value.astype(jnp.bfloat16), "index", scatter_dimension=1, tiled=True
    ).astype(jnp.float32)
    own_states = lax.dynamic_slice_in_dim(states, group_index * quarter, quarter, 1)
    layer = (own_states.astype(jnp.float32) + summed).astype(jnp.bfloat16)
    partial_pool = jnp.dot(member, layer, preferred_element_type=jnp.float32)
    pooled = lax.psum_scatter(
        partial_pool.astype(jnp.bfloat16), "seq", scatter_dimension=0, tiled=True
    ).astype(jnp.float32)
    shard_range = jnp.arange(index_count, dtype=jnp.int32)
    routing = (
        (shard_ids[None, None, :] == shard_range[:, None, None])
        & (slot_rank[None, None, :] == slot_ids[None, :, None])
    ).astype(jnp.float32)
    outgoing = jnp.einsum("rkc,cf->rkf", routing, pooled, precision=lax.Precision.HIGHEST)
    arrived = lax.all_to_all(outgoing, "index", split_axis=0, concat_axis=2, tiled=True)[0]
    shelf_rows = arrived * lax.rsqrt(jnp.mean(arrived * arrived, -1, keepdims=True) + 1e-06)
    return (layer[None], shelf_rows[None, None, None])


def lanes(shape):
    return lax.broadcasted_iota(jnp.int32, shape, 1)


def rotary(tile, cosine, sine):
    first = lanes(tile.shape) % HD < HD // 2
    partner = jnp.where(first, pltpu.roll(tile, 128 - HD // 2, 1), pltpu.roll(tile, HD // 2, 1))
    return tile * cosine + partner * sine


def folded(columns, odd):
    half = columns[0].shape[0] // 2
    low = lanes((half, 128)) < HD
    turn = lambda x: pltpu.roll(x, HD, 1)
    q, k, v = [[c[:half].astype(jnp.float32), c[half:].astype(jnp.float32)] for c in columns]
    parts = [jnp.where(low, jnp.where(odd, turn(q[p]), q[p]), jnp.where(odd, k[p], turn(k[p]))) for p in range(2)]
    parts.append(jnp.where(low, jnp.where(odd, turn(v[0]), v[0]), jnp.where(odd, v[1], turn(v[1]))))
    return jnp.concatenate(parts, 1).astype(columns[0].dtype)


def pieces_kernel(where, w_ref, o_ref, out_ref, first_ref):
    out_ref[...] = o_ref[0]
    first_ref[...] = folded([w_ref[j] for j in range(3)], False)


def pieces(where, proj_weight):
    _, shard, width = proj_weight.shape
    quarter = shard // 4
    return pl.pallas_call(
        pieces_kernel,
        grid_spec=pltpu.PrefetchScalarGridSpec(
            num_scalar_prefetch=1,
            grid=(1,),
            in_specs=[
                pl.BlockSpec((3, shard, 128), lambda i, where: (0, 0, where[0])),
                pl.BlockSpec((1, quarter, width), lambda i, where: (3, where[0], 0)),
            ],
            out_specs=[
                pl.BlockSpec((quarter, width), lambda i, where: (0, 0)),
                pl.BlockSpec((shard // 2, 384), lambda i, where: (0, 0)),
            ],
        ),
        out_shape=[
            jax.ShapeDtypeStruct((quarter, width), proj_weight.dtype),
            jax.ShapeDtypeStruct((shard // 2, 384), proj_weight.dtype),
        ],
        cost_estimate=SHORT,
        name="pieces",
    )(where, proj_weight, proj_weight)


def others_kernel(where, w_ref, x_ref, token_ref, second_ref, third_ref):
    second_ref[...] = folded([w_ref[j] for j in range(3)], True)
    third_ref[...] = folded([x_ref[j] for j in range(3)], lax.rem(where[0], 2) == 1)


def other_pieces(where, proj_weight, token):
    shard = proj_weight.shape[1]
    return pl.pallas_call(
        others_kernel,
        grid_spec=pltpu.PrefetchScalarGridSpec(
            num_scalar_prefetch=1,
            grid=(1,),
            in_specs=[
                pl.BlockSpec((3, shard, 128), lambda i, where: (0, 0, where[0])),
                pl.BlockSpec((3, shard, 128), lambda i, where: (0, 0, 4 + where[0] // 2)),
                pl.BlockSpec(memory_space=pl.ANY),
            ],
            out_specs=[pl.BlockSpec((shard // 2, 384), lambda i, where: (0, 0))] * 2,
        ),
        out_shape=[jax.ShapeDtypeStruct((shard // 2, 384), proj_weight.dtype)] * 2,
        cost_estimate=SHORT,
        name="other_pieces",
    )(where, proj_weight, proj_weight, token)


def after(value, *earlier):
    return lax.optimization_barrier((value, *earlier))[0]


def members(lengths, positions):
    count = lengths.shape[1]
    shape = (count, count)
    row, other = lax.broadcasted_iota(jnp.int32, shape, 0), lax.broadcasted_iota(jnp.int32, shape, 1)
    per_block = count // 4
    stretch = lax.rem(row, per_block) * 4 + row // per_block
    values = jnp.broadcast_to(lengths, shape)
    ends = jnp.sum(jnp.where(other <= stretch, values, 0), 1, keepdims=True)
    starts = jnp.sum(jnp.where(other < stretch, values, 0), 1, keepdims=True)
    position = lax.broadcasted_iota(jnp.int32, (count, positions), 1)
    return jnp.where((position >= starts) & (position < ends), 1.0, 0.0).astype(jnp.bfloat16)


def attend_kernel(pools, *refs):
    where, h_refs, (cos_ref, sin_ref, lengths_ref), w_refs = refs[0], refs[1:5], refs[5:8], refs[8:12]
    out_refs = refs[12:16]
    q_s, k_s, v_s, c_s, member_s = refs[-5:]
    s, d, g = where[0], where[1], where[2]
    rows, d_model = h_refs[0].shape
    total = 4 * rows
    shard = d_model // 4
    half = shard // 2
    per_block = lengths_ref.shape[1] // 4
    member_s[...] = members(lengths_ref[...], total)

    for j in range(4):
        block = jnp.bitwise_xor(s, j)
        at = pl.ds(pl.multiple_of(block * rows, rows), rows)
        top = jnp.zeros((rows, 256), jnp.float32)
        bottom = jnp.zeros((rows, 256), jnp.float32)
        for k in range(4):
            column = lax.rem(d - k + 4, 4) * shard
            w = w_refs[k]
            h_top = h_refs[j][:, pl.ds(pl.multiple_of(column, half), half)]
            h_bottom = h_refs[j][:, pl.ds(pl.multiple_of(column + half, half), half)]
            top += jnp.dot(h_top, jnp.concatenate([w[:, 0:128], w[:, 256:384]], 1), preferred_element_type=jnp.float32)
            bottom += jnp.dot(h_bottom, w[:, 128:384], preferred_element_type=jnp.float32)
        qk = rotary(top[:, :128] + bottom[:, :128], cos_ref[at, :], sin_ref[at, :])
        low = lanes(qk.shape) < HD
        q_s[at, :] = jnp.where(low, qk * HD**-0.5, 0.0).astype(jnp.bfloat16)
        k_s[at, :] = pltpu.roll(qk, HD, 1).astype(jnp.bfloat16)
        v = top[:, 128:] + pltpu.roll(bottom[:, 128:], HD, 1)
        v_s[at, :] = jnp.where(low, v, 1.0).astype(jnp.bfloat16)

    step = 256
    for r in range(total // step):
        start, end = max(0, r * step - HALF_WIN), min(total, (r + 1) * step + HALF_WIN)
        ahead = lax.broadcasted_iota(jnp.int32, (step, step), 1) - lax.broadcasted_iota(jnp.int32, (step, step), 0)
        scores = lax.dot_general(
            q_s[r * step : (r + 1) * step, :], k_s[start:end, :], (((1,), (1,)), ((), ())), preferred_element_type=jnp.float32
        )
        parts = [scores]
        if start == r * step - HALF_WIN:
            parts = [jnp.where(ahead >= 0, scores[:, :step], -1e30), scores[:, step:]]
        if end == (r + 1) * step + HALF_WIN:
            last = parts.pop()
            parts += [last[:, :-step], jnp.where(ahead <= 0, last[:, -step:], -1e30)]
        scores = jnp.concatenate(parts, 1)
        expo = jnp.exp(scores - jnp.max(scores, 1, keepdims=True)).astype(jnp.bfloat16)
        o = jnp.dot(expo, v_s[start:end, :], preferred_element_type=jnp.float32)
        low = lanes(o.shape) < HD
        c_s[r * step : (r + 1) * step, :] = jnp.where(low, o / pltpu.roll(o, HD, 1), 0.0).astype(jnp.bfloat16)

    pooled = jnp.dot(member_s[...], c_s[...], preferred_element_type=jnp.float32)
    high = pooled.astype(jnp.bfloat16)
    rest = (pooled - high.astype(jnp.float32)).astype(jnp.bfloat16)
    for j in range(4):
        block = jnp.bitwise_xor(s, j)
        both = jnp.zeros((2 * per_block, 128), jnp.bfloat16)
        for b in range(4):
            cut = slice(b * per_block, (b + 1) * per_block)
            both = jnp.where(block == b, jnp.concatenate([high[cut], rest[cut]], 0), both)
        out = out_refs[j]
        lo = c_s[pl.ds(pl.multiple_of(block * rows, rows), rows // 2), :].astype(jnp.float32)
        hi = c_s[pl.ds(pl.multiple_of(block * rows + rows // 2, rows // 2), rows // 2), :].astype(jnp.float32)
        out[0 : rows // 2, :] = (lo + pltpu.roll(hi, HD, 1)).astype(jnp.bfloat16)
        out[rows // 2 :, :] = both

    if pools:
        feats = d_model // 2
        sums = jnp.zeros((4 * per_block, feats), jnp.float32)
        for j in range(4):
            rows_of = member_s[:, pl.ds(pl.multiple_of(jnp.bitwise_xor(s, j) * rows, rows), rows)]
            part = h_refs[j][:, pl.ds(pl.multiple_of(g * feats, feats), feats)]
            sums += jnp.dot(rows_of, part, preferred_element_type=jnp.float32)
        own = jnp.zeros((per_block, feats), jnp.float32)
        for b in range(4):
            own = jnp.where(s == b, sums[b * per_block : (b + 1) * per_block], own)
        refs[16][...] = own


def attend(where, blocks, tables, pieces, pools):
    rows, d_model = blocks[0].shape
    total = 4 * rows
    count = tables[2].shape[1]
    per_block = count // 4
    vmem = pl.BlockSpec(memory_space=pltpu.VMEM)
    out_shape = [jax.ShapeDtypeStruct((rows // 2 + 2 * per_block, 128), jnp.bfloat16)] * 4
    if pools:
        out_shape.append(jax.ShapeDtypeStruct((per_block, d_model // 2), jnp.float32))
    return pl.pallas_call(
        functools.partial(attend_kernel, pools),
        out_shape=out_shape,
        in_specs=[pl.BlockSpec(memory_space=pltpu.SMEM)] + [vmem] * 11,
        out_specs=[vmem] * len(out_shape),
        scratch_shapes=[pltpu.VMEM((total, 128), jnp.bfloat16)] * 4 + [pltpu.VMEM((count, total), jnp.bfloat16)],
        compiler_params=pltpu.CompilerParams(vmem_limit_bytes=24 * 2**20),
        cost_estimate=SHORT,
        name="attend_and_pool" if pools else "attend",
    )(where, *blocks, *tables, *pieces)


def merge(left, right, rows):
    left, right = left.astype(jnp.float32), right.astype(jnp.float32)
    low = lanes(left.shape) < HD
    first = jnp.where(low, left, pltpu.roll(right, HD, 1)).astype(jnp.bfloat16)
    second = jnp.where(low, pltpu.roll(left, HD, 1), right).astype(jnp.bfloat16)
    return first[: rows // 2], second[: rows // 2], first[rows // 2 :]


def project_tiles(s, d, c_s, four_ref, near_ref, columns):
    feats, width = four_ref.shape[2], columns[1] - columns[0]
    for p in range(2):
        in_half = lax.rem(lax.rem(d - p + 4, 4), 2)
        for j in range(4):
            source = near_ref if j % 2 else four_ref
            total = None
            for t in range(2):
                w = source[2 * (j // 2) + t, p, :, columns[0] : columns[1]]
                c = c_s[:, t * width : (t + 1) * width]
                product = lax.dot_general(c, w, (((1,), (1,)), ((), ())), preferred_element_type=jnp.float32)
                total = product if total is None else total + product
            yield pl.multiple_of((in_half * 4 + jnp.bitwise_xor(s, j)) * feats, 128), total


def early_kernel(where, *refs):
    firsts, seconds, (four_ref, near_ref, out_ref, c_s) = refs[0:5], refs[5:10], refs[10:]
    s, d = where[0], where[1]
    rows = 2 * (out_ref.shape[0] - firsts[0].shape[0])
    for t in range(2):
        for j in range(4):
            left, right = [r[j][...] if t == 0 else r[4][j] for r in (firsts, seconds)]
            top, bottom, sums = merge(left, right, rows)
            at = pl.ds(pl.multiple_of(t * 512 + jnp.bitwise_xor(s, j) * 128, 128), 128)
            c_s[0 : rows // 2, at] = top
            c_s[rows // 2 : rows, at] = bottom
            c_s[rows:, at] = sums
    for column, total in project_tiles(s, d, c_s, four_ref, near_ref, (0, 512)):
        out_ref[:, pl.ds(column, four_ref.shape[2])] = total


def project_early(where, first, second, weights):
    each = first[0].shape[0]
    feats = 8 * weights[0].shape[2]
    rows = weights[0].shape[2] * 2
    vmem = pl.BlockSpec(memory_space=pltpu.VMEM)
    return pl.pallas_call(
        early_kernel,
        out_shape=jax.ShapeDtypeStruct((each + rows // 2, feats), jnp.float32),
        in_specs=[pl.BlockSpec(memory_space=pltpu.SMEM)] + [vmem] * 12,
        out_specs=vmem,
        scratch_shapes=[pltpu.VMEM((each + rows // 2, 1024), jnp.bfloat16)],
        compiler_params=pltpu.CompilerParams(vmem_limit_bytes=24 * 2**20),
        cost_estimate=SHORT,
        name="project_early",
    )(where, *first, *second, *weights)


def late_kernel(where, shard_ref, h_ref, pool_ref, early_ref, *refs):
    thirds, (four_ref, near_ref, layer_ref, keep_ref, send_ref, c_s, o_s) = refs[0:5], refs[5:]
    s, d, g = where[0], where[1], where[2]
    rows = h_ref.shape[0]
    odd = jnp.bitwise_and(s, 1) == 1
    for t in range(2):
        parts = [thirds[j][...] if t == 0 else thirds[4][j] for j in range(4)]
        for pair in range(2):
            one, two = parts[2 * pair], parts[2 * pair + 1]
            top, bottom, sums = merge(jnp.where(odd, two, one), jnp.where(odd, one, two), rows)
            at = pl.ds(pl.multiple_of(t * 256 + jnp.bitwise_xor(s // 2, pair) * 128, 128), 128)
            c_s[0 : rows // 2, at] = top
            c_s[rows // 2 : rows, at] = bottom
            c_s[rows:, at] = sums

    feats = four_ref.shape[2]
    for column, total in project_tiles(s, d, c_s, four_ref, near_ref, (512, 768)):
        at = pl.ds(column, feats)
        total += early_ref[:, at]
        o_s[:, at] = total[rows:]
        mine = h_ref[:, pl.ds(pl.multiple_of(g * 8 * feats + column, 128), feats)]
        layer_ref[:, at] = (mine.astype(jnp.float32) + total[:rows]).astype(jnp.bfloat16)

    half = pool_ref.shape[0]
    pooled = pool_ref[...] + o_s[0:half] + o_s[half:]
    slots = 2 * keep_ref.shape[0]
    slot = lax.broadcasted_iota(jnp.int32, (slots, half), 0)
    source = lax.broadcasted_iota(jnp.int32, (slots, half), 1)
    route = jnp.zeros((slots, half), jnp.float32)
    ids = [shard_ref[c] for c in range(half)]
    for c in range(half):
        rank = sum([(ids[e] == ids[c]).astype(jnp.int32) for e in range(c)], jnp.int32(0))
        route = jnp.where((slot == ids[c] * (slots // 2) + rank) & (source == c), 1.0, route)
    routed = jnp.dot(route, pooled, precision=lax.Precision.HIGHEST, preferred_element_type=jnp.float32)
    cut = slots // 2
    keep_ref[...] = jnp.where(g == 0, routed[:cut], routed[cut:])
    send_ref[...] = jnp.where(g == 0, routed[cut:], routed[:cut])


def project_late(where, shard_ids, h, pool, early, third, weights):
    rows, d_model = h.shape
    feats = d_model // 2
    slots = shard_ids.shape[0] // 2
    vmem = pl.BlockSpec(memory_space=pltpu.VMEM)
    return pl.pallas_call(
        late_kernel,
        out_shape=[
            jax.ShapeDtypeStruct((rows, feats), jnp.bfloat16),
            jax.ShapeDtypeStruct((slots, feats), jnp.float32),
            jax.ShapeDtypeStruct((slots, feats), jnp.float32),
        ],
        in_specs=[pl.BlockSpec(memory_space=pltpu.SMEM)] * 2 + [vmem] * 10,
        out_specs=[vmem] * 3,
        scratch_shapes=[
            pltpu.VMEM((early.shape[0], 512), jnp.bfloat16),
            pltpu.VMEM((early.shape[0] - rows, feats), jnp.float32),
        ],
        compiler_params=pltpu.CompilerParams(vmem_limit_bytes=24 * 2**20),
        cost_estimate=SHORT,
        name="project_late",
    )(where, shard_ids, h, pool, early, *third, *weights)


def xor_send(name, value, axis, j):
    with jax.named_scope(name):
        return lax.ppermute(value, axis, [(i, i ^ j) for i in range(lax.axis_size(axis))])


def ring_send(name, value):
    count = lax.axis_size("dp")
    with jax.named_scope(name):
        return lax.ppermute(value, "dp", [(i, (i + 1) % count) for i in range(count)])


def rotary_tables(total):
    freqs = np.float32(10000.0) ** (np.float32(-2.0) * np.arange(HD // 2, dtype=np.float32) / np.float32(HD))
    angles = (np.arange(total, dtype=np.float32)[:, None] * freqs[None, :]).astype(np.float64)
    cosine, sine = np.cos(angles).astype(np.float32), np.sin(angles).astype(np.float32)
    return jnp.asarray(np.concatenate([cosine] * 4, 1)), jnp.asarray(np.concatenate([-sine, sine] * 2, 1))


def body_by_heads(hidden, proj_weight, stretch_lengths, shard_of):
    h = hidden[0]
    rows = h.shape[0]
    s, d, g = lax.axis_index("seq"), lax.axis_index("dp"), lax.axis_index("index")
    where = jnp.stack([s, d, g]).astype(jnp.int32)
    total = 4 * rows

    tables = (*rotary_tables(total), stretch_lengths)

    def across(ring):
        pairs = [((d - p) % 4 // 2 == g, ring[p], ring[p + 2]) for p in range(2)]
        keep = jnp.stack([jnp.where(mine, one, two) for mine, one, two in pairs])
        send = jnp.stack([jnp.where(mine, two, one) for mine, one, two in pairs])
        with jax.named_scope("out_across"):
            far = lax.ppermute(send, ("seq", "index"), [(i, i ^ 5) for i in range(8)])
        return keep, xor_send("out_group", send, "index", 1), xor_send("out_cross", keep, "seq", 2), far

    def to_seq(name, parts):
        return [parts[0]] + [xor_send(name, parts[j], "seq", j) for j in (1, 2, 3)]

    def to_other(name, parts):
        return parts + [xor_send(name, jnp.stack(parts), "index", 1)]

    h_cross = xor_send("hidden_cross", h, "seq", 2)
    h_core = xor_send("hidden_core", h, "seq", 1)
    o0, x0 = pieces(where, proj_weight)

    def rings(names, starts, **before):
        held = [[start] for start in starts]
        for step in range(3):
            for ring, name in zip(held, names):
                ring.append(ring_send(name, after(ring[-1], before[name]) if step == 1 and name in before else ring[-1]))
        return held

    out_ring, first_ring = rings(("out", "first"), (o0, x0))
    y0, z0 = other_pieces(where, proj_weight, out_ring[1])
    out_ring[3], first_ring[3], h_core, h_cross, y0, z0 = lax.optimization_barrier(
        (out_ring[3], first_ring[3], h_core, h_cross, y0, z0)
    )

    h_far = xor_send("hidden_far", h_cross, "seq", 1)
    y1, z1 = ring_send("second", y0), ring_send("third", z0)
    y2, z2 = ring_send("second", y1), ring_send("third", after(z1, h_far))
    blocks = [h, h_core, h_cross, h_far]
    four = across(out_ring)
    first_ring[3] = after(first_ring[3], y1, z1)
    first = attend(where, blocks, tables, first_ring, True)
    y3, z3 = ring_send("second", after(y2)), ring_send("third", after(z2, first[4]))
    second_ring, third_ring = [y0, y1, y2, y3], [z0, z1, z2, z3]
    first_parts = to_seq("context_first", first[:4])
    second = attend(where, blocks, tables, second_ring, False)
    third_ring[3], four, first_parts, second = lax.optimization_barrier((third_ring[3], four, first_parts, second))

    four = jnp.stack(four)
    near = xor_send("out_core", four, "seq", 1)
    first_parts = to_other("context_first_group", first_parts)
    second_parts = to_seq("context_second", second)
    third = attend(where, blocks, tables, third_ring, False)
    first_parts, second_parts, third, near = lax.optimization_barrier((first_parts, second_parts, third, near))

    second_parts = to_other("context_second_group", second_parts)
    third_parts = to_seq("context_third", third)
    second_parts[4] = after(second_parts[4], *third_parts)
    third_parts = to_other("context_third_group", third_parts)

    early = project_early(where, first_parts, second_parts, [four, near])
    layer, keep, send = project_late(where, shard_of[0, :, 0], h, first[4], early, third_parts, [four, near])
    arrived = xor_send("embedding_half", send, "index", 1)
    feats = keep.shape[1]
    square = (jnp.sum(keep * keep, -1, keepdims=True) + jnp.sum(arrived * arrived, -1, keepdims=True)) / (2 * feats)
    scale = lax.rsqrt(square + 1e-06)
    shelf = jnp.concatenate([jnp.where(g == 0, keep, arrived), jnp.where(g == 0, arrived, keep)], 1) * scale
    return (layer[None], shelf[None, None, None])


def solution(mesh):
    in_specs = (P("dp", "seq", None), P(None, "dp", "index"), P("dp", None), P("dp", "seq", None))
    out_specs = (P("dp", "seq", "index"), P("dp", "seq", "index", None, None))

    def whole(hidden, proj_weight, stretch_lengths, shard_of):
        heads = proj_weight.shape[2] // HD // mesh.shape["index"]
        rows = hidden.shape[1] // mesh.shape["seq"]
        by_heads = (mesh.shape["dp"], mesh.shape["seq"], mesh.shape["index"], heads, rows) == (4, 4, 2, 12, 256)
        return jax.shard_map(
            body_by_heads if by_heads else body,
            mesh=mesh,
            in_specs=in_specs,
            out_specs=out_specs,
            check_vma=False,
        )(hidden, proj_weight, stretch_lengths, shard_of)

    return whole
```

```python
import functools

import jax
import jax.numpy as jnp
import numpy as np
from jax import lax
from jax.experimental import pallas as pl
from jax.experimental.pallas import tpu as pltpu
from jax.sharding import PartitionSpec as P

D = 2048
HD = 64
HALF_WIN = 256

SHORT = pl.CostEstimate(flops=1, bytes_accessed=1, transcendentals=0)


def with_halo(cells, sides, width):
    for axis, dim in sides:
        count = lax.axis_size(axis)
        ends = count - 1
        head = lax.slice_in_dim(cells, 0, width, axis=dim)
        tail = lax.slice_in_dim(cells, cells.shape[dim] - width, cells.shape[dim], axis=dim)
        cells = jnp.concatenate(
            [
                lax.ppermute(tail, axis, [(i, (i + 1) % count) for i in range(ends)]),
                cells,
                lax.ppermute(head, axis, [((i + 1) % count, i) for i in range(ends)]),
            ],
            axis=dim,
        )
    return cells


def rotate(values_in, positions):
    half_dim = HD // 2
    freqs = 10000.0 ** (-2.0 * jnp.arange(half_dim, dtype=jnp.float32) / HD)
    angles = positions.astype(jnp.float32)[:, None] * freqs[None, :]
    cosine = jnp.cos(angles)[:, None, :]
    sine = jnp.sin(angles)[:, None, :]
    first = values_in[..., :half_dim]
    second = values_in[..., half_dim:]
    return jnp.concatenate([first * cosine - second * sine, second * cosine + first * sine], -1)


def window_heads(queries, key_rows, value_rows, visible):
    scale = HD ** (-0.5)

    def one_head(items):
        query_head, key_head, value_head = items
        scores = jnp.dot(query_head, key_head.T, preferred_element_type=jnp.float32) * scale
        scores = jnp.where(visible, scores, -1e30)
        maxima = jnp.max(scores, -1, keepdims=True)
        expo = jnp.exp(scores - maxima)
        weights = (expo / jnp.sum(expo, -1, keepdims=True)).astype(jnp.bfloat16)
        return jnp.dot(weights, value_head, preferred_element_type=jnp.float32).astype(jnp.bfloat16)

    context = lax.map(
        one_head,
        (jnp.moveaxis(queries, 1, 0), jnp.moveaxis(key_rows, 1, 0), jnp.moveaxis(value_rows, 1, 0)),
    )
    return jnp.moveaxis(context, 0, 1)


def body(hidden, proj_weight, stretch_lengths, shard_of):
    states = hidden[0]
    tokens_here = states.shape[0]
    width = proj_weight.shape[2]
    heads_here = width // HD
    seq_index = lax.axis_index("seq")
    group_index = lax.axis_index("index")
    seq_count = lax.axis_size("seq")
    index_count = lax.axis_size("index")
    total_length = tokens_here * seq_count
    positions = seq_index * tokens_here + jnp.arange(tokens_here, dtype=jnp.int32)
    projected = jnp.einsum(
        "td,jdc->jtc",
        states,
        lax.all_gather(proj_weight[:3], "dp", axis=1, tiled=True),
        preferred_element_type=jnp.float32,
    )
    queries = rotate(projected[0].reshape(tokens_here, heads_here, HD), positions).astype(
        jnp.bfloat16
    )
    key_rows = rotate(projected[1].reshape(tokens_here, heads_here, HD), positions).astype(
        jnp.bfloat16
    )
    value_rows = projected[2].astype(jnp.bfloat16)
    stacked = jnp.stack([key_rows.reshape(tokens_here, width), value_rows])
    padded = with_halo(stacked, (("seq", 1),), HALF_WIN)
    span = tokens_here + 2 * HALF_WIN
    key_part = padded[0, 0:span].reshape(span, heads_here, HD)
    value_part = padded[1, 0:span].reshape(span, heads_here, HD)
    key_pos = seq_index * tokens_here + 0 - HALF_WIN + jnp.arange(span, dtype=jnp.int32)
    visible = (
        (jnp.abs(key_pos[None, :] - positions[:, None]) <= HALF_WIN)
        & (key_pos[None, :] >= 0)
        & (key_pos[None, :] < total_length)
    )
    context_parts = window_heads(queries, key_part, value_part, visible).reshape(tokens_here, width)
    partial_value = lax.dot_general(
        context_parts,
        lax.all_gather(proj_weight[3], "dp", axis=0, tiled=True),
        (((1,), (1,)), ((), ())),
        preferred_element_type=jnp.float32,
    )
    lengths = stretch_lengths[0]
    stretch_count = lengths.shape[0]
    per_block = stretch_count // seq_count
    ends = jnp.cumsum(lengths, dtype=jnp.int32)
    starts = ends - lengths
    row_ids = jnp.arange(stretch_count, dtype=jnp.int32)
    order = row_ids % per_block * seq_count + row_ids // per_block
    row_starts = starts[order]
    row_ends = ends[order]
    member = (
        (positions[None, :] >= row_starts[:, None]) & (positions[None, :] < row_ends[:, None])
    ).astype(jnp.bfloat16)
    shard_ids = shard_of[0, :, 0]
    local_rows = jnp.arange(per_block, dtype=jnp.int32)
    earlier = (shard_ids[:, None] == shard_ids[None, :]) & (
        local_rows[None, :] < local_rows[:, None]
    )
    slot_rank = jnp.sum(earlier.astype(jnp.int32), 1)
    capacity = per_block // 2
    slot_ids = jnp.arange(capacity, dtype=jnp.int32)
    quarter = D // index_count
    summed = lax.psum_scatter(
        partial_value.astype(jnp.bfloat16), "index", scatter_dimension=1, tiled=True
    ).astype(jnp.float32)
    own_states = lax.dynamic_slice_in_dim(states, group_index * quarter, quarter, 1)
    layer = (own_states.astype(jnp.float32) + summed).astype(jnp.bfloat16)
    partial_pool = jnp.dot(member, layer, preferred_element_type=jnp.float32)
    pooled = lax.psum_scatter(
        partial_pool.astype(jnp.bfloat16), "seq", scatter_dimension=0, tiled=True
    ).astype(jnp.float32)
    shard_range = jnp.arange(index_count, dtype=jnp.int32)
    routing = (
        (shard_ids[None, None, :] == shard_range[:, None, None])
        & (slot_rank[None, None, :] == slot_ids[None, :, None])
    ).astype(jnp.float32)
    outgoing = jnp.einsum("rkc,cf->rkf", routing, pooled, precision=lax.Precision.HIGHEST)
    arrived = lax.all_to_all(outgoing, "index", split_axis=0, concat_axis=2, tiled=True)[0]
    shelf_rows = arrived * lax.rsqrt(jnp.mean(arrived * arrived, -1, keepdims=True) + 1e-06)
    return (layer[None], shelf_rows[None, None, None])


def lanes(shape):
    return lax.broadcasted_iota(jnp.int32, shape, 1)


def rotary(tile, cosine, sine):
    first = lanes(tile.shape) % HD < HD // 2
    partner = jnp.where(first, pltpu.roll(tile, 128 - HD // 2, 1), pltpu.roll(tile, HD // 2, 1))
    return tile * cosine + partner * sine


def folded(columns, odd):
    half = columns[0].shape[0] // 2
    low = lanes((half, 128)) < HD
    turn = lambda x: pltpu.roll(x, HD, 1)
    q, k, v = [[c[:half].astype(jnp.float32), c[half:].astype(jnp.float32)] for c in columns]
    parts = [jnp.where(low, jnp.where(odd, turn(q[p]), q[p]), jnp.where(odd, k[p], turn(k[p]))) for p in range(2)]
    parts.append(jnp.where(low, jnp.where(odd, turn(v[0]), v[0]), jnp.where(odd, v[1], turn(v[1]))))
    return jnp.concatenate(parts, 1).astype(columns[0].dtype)


def out_kernel(where, o_ref, out_ref):
    out_ref[...] = o_ref[0]


def out_piece(where, proj_weight):
    _, shard, width = proj_weight.shape
    quarter = shard // 4
    return pl.pallas_call(
        out_kernel,
        grid_spec=pltpu.PrefetchScalarGridSpec(
            num_scalar_prefetch=1,
            grid=(1,),
            in_specs=[pl.BlockSpec((1, quarter, width), lambda i, where: (3, where[0], 0))],
            out_specs=pl.BlockSpec((quarter, width), lambda i, where: (0, 0)),
        ),
        out_shape=jax.ShapeDtypeStruct((quarter, width), proj_weight.dtype),
        cost_estimate=SHORT,
        name="out_piece",
    )(where, proj_weight)


def first_kernel(where, w_ref, token_ref, first_ref):
    first_ref[...] = folded([w_ref[j] for j in range(3)], False)


def first_piece(where, proj_weight, token):
    shard = proj_weight.shape[1]
    return pl.pallas_call(
        first_kernel,
        grid_spec=pltpu.PrefetchScalarGridSpec(
            num_scalar_prefetch=1,
            grid=(1,),
            in_specs=[
                pl.BlockSpec((3, shard, 128), lambda i, where: (0, 0, where[0])),
                pl.BlockSpec(memory_space=pl.ANY),
            ],
            out_specs=pl.BlockSpec((shard // 2, 384), lambda i, where: (0, 0)),
        ),
        out_shape=jax.ShapeDtypeStruct((shard // 2, 384), proj_weight.dtype),
        cost_estimate=SHORT,
        name="first_piece",
    )(where, proj_weight, token)


def others_kernel(where, w_ref, x_ref, token_ref, second_ref, third_ref):
    second_ref[...] = folded([w_ref[j] for j in range(3)], True)
    third_ref[...] = folded([x_ref[j] for j in range(3)], lax.rem(where[0], 2) == 1)


def other_pieces(where, proj_weight, token):
    shard = proj_weight.shape[1]
    return pl.pallas_call(
        others_kernel,
        grid_spec=pltpu.PrefetchScalarGridSpec(
            num_scalar_prefetch=1,
            grid=(1,),
            in_specs=[
                pl.BlockSpec((3, shard, 128), lambda i, where: (0, 0, where[0])),
                pl.BlockSpec((3, shard, 128), lambda i, where: (0, 0, 4 + where[0] // 2)),
                pl.BlockSpec(memory_space=pl.ANY),
            ],
            out_specs=[pl.BlockSpec((shard // 2, 384), lambda i, where: (0, 0))] * 2,
        ),
        out_shape=[jax.ShapeDtypeStruct((shard // 2, 384), proj_weight.dtype)] * 2,
        cost_estimate=SHORT,
        name="other_pieces",
    )(where, proj_weight, proj_weight, token)


def after(value, *earlier):
    return lax.optimization_barrier((value, *earlier))[0]


def members(lengths, positions):
    count = lengths.shape[1]
    shape = (count, count)
    row, other = lax.broadcasted_iota(jnp.int32, shape, 0), lax.broadcasted_iota(jnp.int32, shape, 1)
    per_block = count // 4
    stretch = lax.rem(row, per_block) * 4 + row // per_block
    values = jnp.broadcast_to(lengths, shape)
    ends = jnp.sum(jnp.where(other <= stretch, values, 0), 1, keepdims=True)
    starts = jnp.sum(jnp.where(other < stretch, values, 0), 1, keepdims=True)
    position = lax.broadcasted_iota(jnp.int32, (count, positions), 1)
    return jnp.where((position >= starts) & (position < ends), 1.0, 0.0).astype(jnp.bfloat16)


def attend_kernel(pools, *refs):
    where, h_refs, (cos_ref, sin_ref, lengths_ref), w_refs = refs[0], refs[1:5], refs[5:8], refs[8:12]
    out_refs = refs[12:16]
    q_s, k_s, v_s, c_s, member_s = refs[-5:]
    s, d, g = where[0], where[1], where[2]
    rows, d_model = h_refs[0].shape
    total = 4 * rows
    shard = d_model // 4
    half = shard // 2
    per_block = lengths_ref.shape[1] // 4
    member_s[...] = members(lengths_ref[...], total)

    for j in range(4):
        block = jnp.bitwise_xor(s, j)
        at = pl.ds(pl.multiple_of(block * rows, rows), rows)
        top = jnp.zeros((rows, 256), jnp.float32)
        bottom = jnp.zeros((rows, 256), jnp.float32)
        for k in range(4):
            column = lax.rem(d - k + 4, 4) * shard
            w = w_refs[k]
            h_top = h_refs[j][:, pl.ds(pl.multiple_of(column, half), half)]
            h_bottom = h_refs[j][:, pl.ds(pl.multiple_of(column + half, half), half)]
            top += jnp.dot(h_top, jnp.concatenate([w[:, 0:128], w[:, 256:384]], 1), preferred_element_type=jnp.float32)
            bottom += jnp.dot(h_bottom, w[:, 128:384], preferred_element_type=jnp.float32)
        qk = rotary(top[:, :128] + bottom[:, :128], cos_ref[at, :], sin_ref[at, :])
        low = lanes(qk.shape) < HD
        q_s[at, :] = jnp.where(low, qk * HD**-0.5, 0.0).astype(jnp.bfloat16)
        k_s[at, :] = pltpu.roll(qk, HD, 1).astype(jnp.bfloat16)
        v = top[:, 128:] + pltpu.roll(bottom[:, 128:], HD, 1)
        v_s[at, :] = jnp.where(low, v, 1.0).astype(jnp.bfloat16)

    step = 256
    for r in range(total // step):
        start, end = max(0, r * step - HALF_WIN), min(total, (r + 1) * step + HALF_WIN)
        ahead = lax.broadcasted_iota(jnp.int32, (step, step), 1) - lax.broadcasted_iota(jnp.int32, (step, step), 0)
        scores = lax.dot_general(
            q_s[r * step : (r + 1) * step, :], k_s[start:end, :], (((1,), (1,)), ((), ())), preferred_element_type=jnp.float32
        )
        parts = [scores]
        if start == r * step - HALF_WIN:
            parts = [jnp.where(ahead >= 0, scores[:, :step], -1e30), scores[:, step:]]
        if end == (r + 1) * step + HALF_WIN:
            last = parts.pop()
            parts += [last[:, :-step], jnp.where(ahead <= 0, last[:, -step:], -1e30)]
        scores = jnp.concatenate(parts, 1)
        expo = jnp.exp(scores - jnp.max(scores, 1, keepdims=True)).astype(jnp.bfloat16)
        o = jnp.dot(expo, v_s[start:end, :], preferred_element_type=jnp.float32)
        low = lanes(o.shape) < HD
        c_s[r * step : (r + 1) * step, :] = jnp.where(low, o / pltpu.roll(o, HD, 1), 0.0).astype(jnp.bfloat16)

    pooled = jnp.dot(member_s[...], c_s[...], preferred_element_type=jnp.float32)
    high = pooled.astype(jnp.bfloat16)
    rest = (pooled - high.astype(jnp.float32)).astype(jnp.bfloat16)
    for j in range(4):
        block = jnp.bitwise_xor(s, j)
        both = jnp.zeros((2 * per_block, 128), jnp.bfloat16)
        for b in range(4):
            cut = slice(b * per_block, (b + 1) * per_block)
            both = jnp.where(block == b, jnp.concatenate([high[cut], rest[cut]], 0), both)
        out = out_refs[j]
        lo = c_s[pl.ds(pl.multiple_of(block * rows, rows), rows // 2), :].astype(jnp.float32)
        hi = c_s[pl.ds(pl.multiple_of(block * rows + rows // 2, rows // 2), rows // 2), :].astype(jnp.float32)
        out[0 : rows // 2, :] = (lo + pltpu.roll(hi, HD, 1)).astype(jnp.bfloat16)
        out[rows // 2 :, :] = both

    if pools:
        feats = d_model // 2
        sums = jnp.zeros((4 * per_block, feats), jnp.float32)
        for j in range(4):
            rows_of = member_s[:, pl.ds(pl.multiple_of(jnp.bitwise_xor(s, j) * rows, rows), rows)]
            part = h_refs[j][:, pl.ds(pl.multiple_of(g * feats, feats), feats)]
            sums += jnp.dot(rows_of, part, preferred_element_type=jnp.float32)
        own = jnp.zeros((per_block, feats), jnp.float32)
        for b in range(4):
            own = jnp.where(s == b, sums[b * per_block : (b + 1) * per_block], own)
        refs[16][...] = own


def attend(where, blocks, tables, pieces, pools):
    rows, d_model = blocks[0].shape
    total = 4 * rows
    count = tables[2].shape[1]
    per_block = count // 4
    vmem = pl.BlockSpec(memory_space=pltpu.VMEM)
    out_shape = [jax.ShapeDtypeStruct((rows // 2 + 2 * per_block, 128), jnp.bfloat16)] * 4
    if pools:
        out_shape.append(jax.ShapeDtypeStruct((per_block, d_model // 2), jnp.float32))
    return pl.pallas_call(
        functools.partial(attend_kernel, pools),
        out_shape=out_shape,
        in_specs=[pl.BlockSpec(memory_space=pltpu.SMEM)] + [vmem] * 11,
        out_specs=[vmem] * len(out_shape),
        scratch_shapes=[pltpu.VMEM((total, 128), jnp.bfloat16)] * 4 + [pltpu.VMEM((count, total), jnp.bfloat16)],
        compiler_params=pltpu.CompilerParams(vmem_limit_bytes=24 * 2**20),
        cost_estimate=SHORT,
        name="attend_and_pool" if pools else "attend",
    )(where, *blocks, *tables, *pieces)


def merge(left, right, rows):
    left, right = left.astype(jnp.float32), right.astype(jnp.float32)
    low = lanes(left.shape) < HD
    first = jnp.where(low, left, pltpu.roll(right, HD, 1)).astype(jnp.bfloat16)
    second = jnp.where(low, pltpu.roll(left, HD, 1), right).astype(jnp.bfloat16)
    return first[: rows // 2], second[: rows // 2], first[rows // 2 :]


def project_tiles(s, d, c_s, four_ref, near_ref, columns):
    feats, width = four_ref.shape[2], columns[1] - columns[0]
    for p in range(2):
        in_half = lax.rem(lax.rem(d - p + 4, 4), 2)
        for j in range(4):
            source = near_ref if j % 2 else four_ref
            total = None
            for t in range(2):
                w = source[2 * (j // 2) + t, p, :, columns[0] : columns[1]]
                c = c_s[:, t * width : (t + 1) * width]
                product = lax.dot_general(c, w, (((1,), (1,)), ((), ())), preferred_element_type=jnp.float32)
                total = product if total is None else total + product
            yield pl.multiple_of((in_half * 4 + jnp.bitwise_xor(s, j)) * feats, 128), total


def early_kernel(where, *refs):
    firsts, seconds, (four_ref, near_ref, out_ref, c_s) = refs[0:5], refs[5:10], refs[10:]
    s, d = where[0], where[1]
    rows = 2 * (out_ref.shape[0] - firsts[0].shape[0])
    for t in range(2):
        for j in range(4):
            left, right = [r[j][...] if t == 0 else r[4][j] for r in (firsts, seconds)]
            top, bottom, sums = merge(left, right, rows)
            at = pl.ds(pl.multiple_of(t * 512 + jnp.bitwise_xor(s, j) * 128, 128), 128)
            c_s[0 : rows // 2, at] = top
            c_s[rows // 2 : rows, at] = bottom
            c_s[rows:, at] = sums
    for column, total in project_tiles(s, d, c_s, four_ref, near_ref, (0, 512)):
        out_ref[:, pl.ds(column, four_ref.shape[2])] = total


def project_early(where, first, second, weights):
    each = first[0].shape[0]
    feats = 8 * weights[0].shape[2]
    rows = weights[0].shape[2] * 2
    vmem = pl.BlockSpec(memory_space=pltpu.VMEM)
    return pl.pallas_call(
        early_kernel,
        out_shape=jax.ShapeDtypeStruct((each + rows // 2, feats), jnp.float32),
        in_specs=[pl.BlockSpec(memory_space=pltpu.SMEM)] + [vmem] * 12,
        out_specs=vmem,
        scratch_shapes=[pltpu.VMEM((each + rows // 2, 1024), jnp.bfloat16)],
        compiler_params=pltpu.CompilerParams(vmem_limit_bytes=24 * 2**20),
        cost_estimate=SHORT,
        name="project_early",
    )(where, *first, *second, *weights)


def late_kernel(where, shard_ref, h_ref, pool_ref, early_ref, *refs):
    thirds, (four_ref, near_ref, layer_ref, keep_ref, send_ref, c_s, o_s) = refs[0:5], refs[5:]
    s, d, g = where[0], where[1], where[2]
    rows = h_ref.shape[0]
    odd = jnp.bitwise_and(s, 1) == 1
    for t in range(2):
        parts = [thirds[j][...] if t == 0 else thirds[4][j] for j in range(4)]
        for pair in range(2):
            one, two = parts[2 * pair], parts[2 * pair + 1]
            top, bottom, sums = merge(jnp.where(odd, two, one), jnp.where(odd, one, two), rows)
            at = pl.ds(pl.multiple_of(t * 256 + jnp.bitwise_xor(s // 2, pair) * 128, 128), 128)
            c_s[0 : rows // 2, at] = top
            c_s[rows // 2 : rows, at] = bottom
            c_s[rows:, at] = sums

    feats = four_ref.shape[2]
    for column, total in project_tiles(s, d, c_s, four_ref, near_ref, (512, 768)):
        at = pl.ds(column, feats)
        total += early_ref[:, at]
        o_s[:, at] = total[rows:]
        mine = h_ref[:, pl.ds(pl.multiple_of(g * 8 * feats + column, 128), feats)]
        layer_ref[:, at] = (mine.astype(jnp.float32) + total[:rows]).astype(jnp.bfloat16)

    half = pool_ref.shape[0]
    pooled = pool_ref[...] + o_s[0:half] + o_s[half:]
    slots = 2 * keep_ref.shape[0]
    slot = lax.broadcasted_iota(jnp.int32, (slots, half), 0)
    source = lax.broadcasted_iota(jnp.int32, (slots, half), 1)
    route = jnp.zeros((slots, half), jnp.float32)
    ids = [shard_ref[c] for c in range(half)]
    for c in range(half):
        rank = sum([(ids[e] == ids[c]).astype(jnp.int32) for e in range(c)], jnp.int32(0))
        route = jnp.where((slot == ids[c] * (slots // 2) + rank) & (source == c), 1.0, route)
    routed = jnp.dot(route, pooled, precision=lax.Precision.HIGHEST, preferred_element_type=jnp.float32)
    cut = slots // 2
    keep_ref[...] = jnp.where(g == 0, routed[:cut], routed[cut:])
    send_ref[...] = jnp.where(g == 0, routed[cut:], routed[:cut])


def project_late(where, shard_ids, h, pool, early, third, weights):
    rows, d_model = h.shape
    feats = d_model // 2
    slots = shard_ids.shape[0] // 2
    vmem = pl.BlockSpec(memory_space=pltpu.VMEM)
    return pl.pallas_call(
        late_kernel,
        out_shape=[
            jax.ShapeDtypeStruct((rows, feats), jnp.bfloat16),
            jax.ShapeDtypeStruct((slots, feats), jnp.float32),
            jax.ShapeDtypeStruct((slots, feats), jnp.float32),
        ],
        in_specs=[pl.BlockSpec(memory_space=pltpu.SMEM)] * 2 + [vmem] * 10,
        out_specs=[vmem] * 3,
        scratch_shapes=[
            pltpu.VMEM((early.shape[0], 512), jnp.bfloat16),
            pltpu.VMEM((early.shape[0] - rows, feats), jnp.float32),
        ],
        compiler_params=pltpu.CompilerParams(vmem_limit_bytes=24 * 2**20),
        cost_estimate=SHORT,
        name="project_late",
    )(where, shard_ids, h, pool, early, *third, *weights)


def xor_send(name, value, axis, j):
    with jax.named_scope(name):
        return lax.ppermute(value, axis, [(i, i ^ j) for i in range(lax.axis_size(axis))])


def ring_send(name, value):
    count = lax.axis_size("dp")
    with jax.named_scope(name):
        return lax.ppermute(value, "dp", [(i, (i + 1) % count) for i in range(count)])


def rotary_tables(total):
    freqs = np.float32(10000.0) ** (np.float32(-2.0) * np.arange(HD // 2, dtype=np.float32) / np.float32(HD))
    angles = (np.arange(total, dtype=np.float32)[:, None] * freqs[None, :]).astype(np.float64)
    cosine, sine = np.cos(angles).astype(np.float32), np.sin(angles).astype(np.float32)
    return jnp.asarray(np.concatenate([cosine] * 4, 1)), jnp.asarray(np.concatenate([-sine, sine] * 2, 1))


def body_by_heads(hidden, proj_weight, stretch_lengths, shard_of):
    h = hidden[0]
    rows = h.shape[0]
    s, d, g = lax.axis_index("seq"), lax.axis_index("dp"), lax.axis_index("index")
    where = jnp.stack([s, d, g]).astype(jnp.int32)
    total = 4 * rows

    tables = (*rotary_tables(total), stretch_lengths)

    def across(ring):
        pairs = [((d - p) % 4 // 2 == g, ring[p], ring[p + 2]) for p in range(2)]
        keep = jnp.stack([jnp.where(mine, one, two) for mine, one, two in pairs])
        send = jnp.stack([jnp.where(mine, two, one) for mine, one, two in pairs])
        with jax.named_scope("out_across"):
            far = lax.ppermute(send, ("seq", "index"), [(i, i ^ 5) for i in range(8)])
        return keep, xor_send("out_group", send, "index", 1), xor_send("out_cross", keep, "seq", 2), far

    def to_seq(name, parts):
        return [parts[0]] + [xor_send(name, parts[j], "seq", j) for j in (1, 2, 3)]

    def to_other(name, parts):
        return parts + [xor_send(name, jnp.stack(parts), "index", 1)]

    h_cross = xor_send("hidden_cross", h, "seq", 2)
    h_core = xor_send("hidden_core", h, "seq", 1)
    o0 = out_piece(where, proj_weight)
    x0 = first_piece(where, proj_weight, o0)

    def rings(names, starts, **before):
        held = [[start] for start in starts]
        for step in range(3):
            for ring, name in zip(held, names):
                ring.append(ring_send(name, after(ring[-1], before[name]) if step == 1 and name in before else ring[-1]))
        return held

    out_ring, first_ring = rings(("out", "first"), (o0, x0))
    y0, z0 = other_pieces(where, proj_weight, out_ring[1])
    out_ring[3], first_ring[3], h_core, h_cross, y0, z0 = lax.optimization_barrier(
        (out_ring[3], first_ring[3], h_core, h_cross, y0, z0)
    )

    h_far = xor_send("hidden_far", h_cross, "seq", 1)
    y1, z1 = ring_send("second", y0), ring_send("third", z0)
    y2, z2 = ring_send("second", y1), ring_send("third", after(z1, h_far))
    blocks = [h, h_core, h_cross, h_far]
    four = across(out_ring)
    first_ring[3] = after(first_ring[3], y1, z1)
    first = attend(where, blocks, tables, first_ring, True)
    y3, z3 = ring_send("second", after(y2)), ring_send("third", after(z2, first[4]))
    second_ring, third_ring = [y0, y1, y2, y3], [z0, z1, z2, z3]
    first_parts = to_seq("context_first", first[:4])
    second = attend(where, blocks, tables, second_ring, False)
    third_ring[3], four, first_parts, second = lax.optimization_barrier((third_ring[3], four, first_parts, second))

    four = jnp.stack(four)
    near = xor_send("out_core", four, "seq", 1)
    first_parts = to_other("context_first_group", first_parts)
    second_parts = to_seq("context_second", second)
    third = attend(where, blocks, tables, third_ring, False)
    first_parts, second_parts, third, near = lax.optimization_barrier((first_parts, second_parts, third, near))

    second_parts = to_other("context_second_group", second_parts)
    third_parts = to_seq("context_third", third)
    second_parts[4] = after(second_parts[4], *third_parts)
    third_parts = to_other("context_third_group", third_parts)

    early = project_early(where, first_parts, second_parts, [four, near])
    layer, keep, send = project_late(where, shard_of[0, :, 0], h, first[4], early, third_parts, [four, near])
    arrived = xor_send("embedding_half", send, "index", 1)
    feats = keep.shape[1]
    square = (jnp.sum(keep * keep, -1, keepdims=True) + jnp.sum(arrived * arrived, -1, keepdims=True)) / (2 * feats)
    scale = lax.rsqrt(square + 1e-06)
    shelf = jnp.concatenate([jnp.where(g == 0, keep, arrived), jnp.where(g == 0, arrived, keep)], 1) * scale
    return (layer[None], shelf[None, None, None])


def solution(mesh):
    in_specs = (P("dp", "seq", None), P(None, "dp", "index"), P("dp", None), P("dp", "seq", None))
    out_specs = (P("dp", "seq", "index"), P("dp", "seq", "index", None, None))

    def whole(hidden, proj_weight, stretch_lengths, shard_of):
        heads = proj_weight.shape[2] // HD // mesh.shape["index"]
        rows = hidden.shape[1] // mesh.shape["seq"]
        by_heads = (mesh.shape["dp"], mesh.shape["seq"], mesh.shape["index"], heads, rows) == (4, 4, 2, 12, 256)
        return jax.shard_map(
            body_by_heads if by_heads else body,
            mesh=mesh,
            in_specs=in_specs,
            out_specs=out_specs,
            check_vma=False,
        )(hidden, proj_weight, stretch_lengths, shard_of)

    return whole
```
